256 devices in a mesh: frame: 16 (over y, x), pixel: 16 (over z, core).
Axes of the slice: x: 4, y: 4, z: 8, core: 2. Of those that a mesh axis runs over, the one named last changes fastest.
Arguments:
- tokens: bfloat16 [16, 512, 2048], P('frame', 'pixel'), may hold values from -20 to 20
- spatial_inputs: bfloat16 [16, 512, 6144], P('frame', 'pixel'), may hold values from -6 to 6
- temporal_inputs: bfloat16 [16, 512, 6144], P('frame', 'pixel'), may hold values from -6 to 6
- gate_spatial: float32 [2048], replicated, may hold values from 1 to 4
- gate_temporal: float32 [2048], replicated, may hold values from 1 to 4
- norm_gain: float32 [2048], replicated, may hold values from 0.1 to 1.9
- route_experts: int32 [16, 512, 6], P('frame', 'pixel'), may hold values from 0 to 63, as said below
- route_weights: float32 [16, 512, 6], P('frame', 'pixel'), may hold values from 0.1 to 0.6
- expert_gate_up: bfloat16 [256, 2048, 704], P(('frame', 'pixel')), may hold values from -0.125 to 0.125
- expert_down: bfloat16 [256, 352, 2048], P(('frame', 'pixel')), may hold values from -0.15625 to 0.15625
Outputs:
- attended: bfloat16 [16, 512, 2048], P('frame', 'pixel')
- expert_mix: bfloat16 [16, 512, 2048], P('frame', 'pixel')
The draws below stay inside these ranges and needn't reach their ends.
Inputs may be any that keep to these rules, and one draw needn't show every extreme that they name: `route_experts`: each row names 6 different experts. Within one frame, each aligned block of 32 positions names any one expert at most 8 times, and in every such block some experts exactly 8 times.
All inputs are finite; a program needn't handle non-finite values.
Results may differ from the reference program's by a relative error of at most 0.02.
Values may be sent and summed in bfloat16 or wider, within the bound.
A program may use at most 64 MiB of HBM per device.

```python
import math
import jax
import jax.numpy as jnp
from jax import lax

D = 2048
HEADS = 16
HDIM = 128
FF = 1408
TOP = 6
EXP_COL = 4
PIX_DEV = 32
INNER = 2048
EXPERTS = 64
MOST = 8
SLICES = 4
FF_SLICE = 352
BLOCKS = 256
FRAMES = 16
PIXELS = 512


def distinct_order(noise_key, rows_count, length):
    ranked = jax.random.randint(noise_key, (rows_count, length), 0, 1 << 20) * length + jnp.arange(length)
    return jnp.argsort(ranked, axis=1).astype(jnp.int32)


def draw_tokens(key, part):
    key = jax.random.fold_in(key, 7)
    noise_key = jax.random.fold_in(key, 0)
    layout = (FRAMES, PIXELS, D)
    values = jax.random.truncated_normal(noise_key, -6.0, 6.0, layout, jnp.float32)
    return values.astype(jnp.bfloat16)


def draw_spatial_inputs(key, part):
    key = jax.random.fold_in(key, 3)
    base_key = jax.random.fold_in(key, 0)
    layout = (FRAMES, PIXELS, 3, HEADS, HDIM)
    values = 1.3 * jax.random.truncated_normal(base_key, -6.0 / 1.3, 6.0 / 1.3, layout, jnp.float32)
    return values.reshape(FRAMES, PIXELS, 3 * INNER).astype(jnp.bfloat16)


def draw_temporal_inputs(key, part):
    key = jax.random.fold_in(key, 5)
    base_key = jax.random.fold_in(key, 0)
    layout = (FRAMES, PIXELS, 3, HEADS, HDIM)
    values = 1.3 * jax.random.truncated_normal(base_key, -6.0 / 1.3, 6.0 / 1.3, layout, jnp.float32)
    return values.reshape(FRAMES, PIXELS, 3 * INNER).astype(jnp.bfloat16)


def draw_route_experts(key, part):
    key = jax.random.fold_in(key, 11)
    global_key, others_key, sequence_key, rows_key = jax.random.split(key, 4)
    block_count = FRAMES * (PIXELS // PIX_DEV)
    slot_count = PIX_DEV * TOP
    remaining = EXPERTS - TOP
    leftover = slot_count - TOP * MOST
    base_count = leftover // remaining
    extra_count = leftover % remaining
    ordering = distinct_order(global_key, 1, EXPERTS)[0]
    busy_experts = ordering[:TOP]
    other_experts = ordering[TOP:]
    other_order = distinct_order(others_key, block_count, remaining)
    others_block = other_experts[other_order]
    other_counts = base_count + (jnp.arange(remaining) < extra_count).astype(jnp.int32)
    expert_table = jnp.concatenate([jnp.broadcast_to(busy_experts[None, :], (block_count, TOP)), others_block], axis=1)
    count_table = jnp.concatenate([jnp.full((block_count, TOP), MOST, jnp.int32), jnp.broadcast_to(other_counts[None, :], (block_count, remaining))], axis=1)
    sequence_order = distinct_order(sequence_key, block_count, EXPERTS)
    expert_sequence = jnp.take_along_axis(expert_table, sequence_order, axis=1)
    count_sequence = jnp.take_along_axis(count_table, sequence_order, axis=1)
    run_ends = jnp.cumsum(count_sequence, axis=1)
    positions = jnp.arange(slot_count, dtype=jnp.int32)
    run_index = jnp.sum((run_ends[:, None, :] <= positions[None, :, None]).astype(jnp.int32), axis=-1)
    filled = jnp.take_along_axis(expert_sequence, run_index, axis=1)
    grid = jnp.transpose(filled.reshape(block_count, TOP, PIX_DEV), (0, 2, 1))
    row_order = distinct_order(rows_key, block_count, PIX_DEV)
    grid = jnp.take_along_axis(grid, row_order[:, :, None], axis=1)
    return grid.reshape(FRAMES, PIXELS, TOP).astype(jnp.int32)


def levels(own_key, shape, cuts, least, largest):
    gain = 1.0
    for position, parts in cuts:
        heights = jax.random.uniform(jax.random.fold_in(jax.random.fold_in(own_key, 6), position), (parts,), jnp.float32, least / len(cuts), largest / len(cuts))
        gain = gain * jnp.repeat(jnp.exp(heights), shape[position] // parts).reshape((-1,) + (1,) * (len(shape) - 1 - position))
    return gain


def noise(stream_key, extent, deviation, bound, shards=(), held_as=jnp.bfloat16):
    entries = jax.random.normal(stream_key, extent, jnp.float32) * deviation
    if len(shards) > 0:
        entries = levels(stream_key, extent, shards, -0.22, 0.18) * entries
    return jnp.clip(entries, min=-bound, max=bound).astype(held_as)


def setup_inputs(seed: int = 0) -> dict:
    splits = jax.random.split(jax.random.key(seed), 11)
    tokens = draw_tokens(jax.random.fold_in(splits[10], 71), 0)
    spatial_inputs = draw_spatial_inputs(jax.random.fold_in(splits[10], 71), 0)
    temporal_inputs = draw_temporal_inputs(jax.random.fold_in(splits[10], 71), 0)
    gate_spatial = jnp.clip(jnp.exp(jax.random.uniform(splits[3], (D,), jnp.float32, math.log(1.0), math.log(4.0))), 1.0, 4.0)
    gate_temporal = jnp.clip(jnp.exp(jax.random.uniform(splits[4], (D,), jnp.float32, math.log(1.0), math.log(4.0))), 1.0, 4.0)
    norm_gain = jnp.clip(1.0 + 0.18 * jax.random.normal(splits[5], (D,), jnp.float32), 0.1, 1.9)
    route_experts = draw_route_experts(jax.random.fold_in(splits[10], 71), 0)
    route_weights = jnp.clip(0.1 + 0.5 * jax.random.uniform(splits[7], (FRAMES, PIXELS, TOP), jnp.float32) ** levels(splits[7], (FRAMES, PIXELS, TOP), ((0, 16), (1, 16)), -0.2, 0.2), 0.1, 0.6)
    expert_gate_up = noise(splits[8], (BLOCKS, D, 2 * FF_SLICE), D ** -0.5, 0.125, ((0, 256),))
    expert_down = noise(splits[9], (BLOCKS, FF_SLICE, D), FF ** -0.5, 0.15625, ((0, 256),))
    return {"tokens": tokens, "spatial_inputs": spatial_inputs, "temporal_inputs": temporal_inputs, "gate_spatial": gate_spatial, "gate_temporal": gate_temporal, "norm_gain": norm_gain, "route_experts": route_experts, "route_weights": route_weights, "expert_gate_up": expert_gate_up, "expert_down": expert_down}


def attend(queries, key_rows, values):
    divisor = math.sqrt(queries.shape[-1])
    scores = jnp.einsum('bqhd,bkhd->bhqk', queries.astype(jnp.float32), key_rows.astype(jnp.float32), precision=lax.Precision.HIGHEST) / divisor
    row_max = lax.optimization_barrier(jnp.max(scores, axis=-1, keepdims=True))
    weights = jnp.exp(scores - row_max)
    row_total = lax.optimization_barrier(jnp.sum(weights, axis=-1))
    rounded = weights.astype(jnp.bfloat16)
    output = jnp.einsum('bhqk,bkhd->bqhd', rounded.astype(jnp.float32), values.astype(jnp.float32), precision=lax.Precision.HIGHEST)
    return (output / jnp.transpose(row_total, (0, 2, 1))[..., None]).astype(jnp.bfloat16)

def spatial_frame(packed_frame):
    return attend(packed_frame[None, :, 0], packed_frame[None, :, 1], packed_frame[None, :, 2])[0]

def reference(tokens, spatial_inputs, temporal_inputs, gate_spatial, gate_temporal, norm_gain, route_experts, route_weights, expert_gate_up, expert_down):
    packed = spatial_inputs.reshape(FRAMES, PIXELS, 3, HEADS, HDIM)
    spatial = lax.map(spatial_frame, packed).reshape(FRAMES, PIXELS, INNER)
    by_pixel = jnp.swapaxes(temporal_inputs.reshape(FRAMES, PIXELS, 3, HEADS, HDIM), 0, 1)
    temporal = jnp.swapaxes(attend(by_pixel[:, :, 0], by_pixel[:, :, 1], by_pixel[:, :, 2]), 0, 1).reshape(FRAMES, PIXELS, INNER)
    combined = tokens.astype(jnp.float32) + gate_spatial * spatial.astype(jnp.float32) + gate_temporal * temporal.astype(jnp.float32)
    attended = combined.astype(jnp.bfloat16)
    widened = attended.astype(jnp.float32)
    mean_square = lax.optimization_barrier(jnp.mean(widened * widened, axis=-1, keepdims=True))
    expert_input = (widened * lax.rsqrt(mean_square + 1e-06) * norm_gain).astype(jnp.bfloat16).reshape(FRAMES * PIXELS, D)
    flat_experts = route_experts.reshape(-1).astype(jnp.int32)
    flat_weights = route_weights.reshape(-1)
    assigned = flat_experts.shape[0]
    capacity = FRAMES * PIXELS // PIX_DEV * MOST
    columns = EXPERTS // EXP_COL
    slice_index = jnp.arange(SLICES, dtype=jnp.int32)

    def one_expert(mixture, expert):
        column = expert // EXP_COL
        within = expert % EXP_COL
        blocks = ((within * SLICES + slice_index) * columns + column).astype(jnp.int32)
        gate_up = expert_gate_up[blocks].astype(jnp.float32)
        down_rows = expert_down[blocks].astype(jnp.float32)
        found_at = jnp.nonzero(flat_experts == expert, size=capacity, fill_value=assigned)[0].astype(jnp.int32)
        is_valid = found_at < assigned
        safe_at = jnp.minimum(found_at, assigned - 1)
        token_rows = safe_at // TOP
        row_scale = jnp.where(is_valid, flat_weights[safe_at], jnp.zeros_like(flat_weights[safe_at]))
        rows_in = expert_input[token_rows].astype(jnp.float32)
        gate_and_up = jnp.einsum('rd,sdf->rsf', rows_in, gate_up, precision=lax.Precision.HIGHEST)
        active = (jax.nn.silu(gate_and_up[..., :FF_SLICE]) * gate_and_up[..., FF_SLICE:]).astype(jnp.bfloat16)
        slice_parts = jnp.einsum('rsf,sfd->rsd', active.astype(jnp.float32), down_rows, precision=lax.Precision.HIGHEST).astype(jnp.bfloat16)
        result = lax.optimization_barrier(jnp.sum(slice_parts.astype(jnp.float32), axis=1)).astype(jnp.bfloat16)
        mixture = mixture.at[token_rows].add(row_scale[:, None] * result.astype(jnp.float32))
        return (mixture, None)
    mixture, unused = lax.scan(one_expert, jnp.zeros((FRAMES * PIXELS, D), jnp.float32), jnp.arange(EXPERTS, dtype=jnp.int32))
    expert_mix = mixture.reshape(FRAMES, PIXELS, D).astype(jnp.bfloat16)
    return (attended, expert_mix)
```

```python
import math

import jax
import jax.numpy as jnp
from jax import lax
from jax.sharding import PartitionSpec as P

HEADS = 16
HDIM = 128
TOP = 6
CAP = 8
SIDE = 4


def attend(queries, key_rows, values, same=None):
    divisor = math.sqrt(queries.shape[-1])
    scores = jnp.dot(queries, key_rows.T, preferred_element_type=jnp.float32) / divisor
    if same is not None:
        scores = jnp.where(same, scores, -1e30)
    row_max = jnp.max(scores, axis=-1, keepdims=True)
    weights = jnp.exp(scores - row_max)
    row_total = jnp.sum(weights, axis=-1, keepdims=True)
    output = jnp.dot(weights.astype(jnp.bfloat16), values, preferred_element_type=jnp.float32)
    return (output / row_total).astype(jnp.bfloat16)


def per_device(
    tokens,
    spatial_inputs,
    temporal_inputs,
    gate_spatial,
    gate_temporal,
    norm_gain,
    route_experts,
    route_weights,
    expert_gate_up,
    expert_down,
):
    model_width = tokens.shape[-1]
    here = tokens.shape[1]
    frames = lax.axis_size("frame")
    columns = lax.axis_size("pixel")
    ff = expert_down.shape[1]
    half = ff // 2

    def shift(dx):
        return [(f, f // SIDE * SIDE + (f % SIDE + dx) % SIDE) for f in range(frames)]

    gate, up, down = expert_gate_up[0, :, :ff], expert_gate_up[0, :, ff:], expert_down[0]
    piece_a = jnp.concatenate([gate[:, :half], up[:, :half]], axis=1)
    piece_b = jnp.concatenate([gate[:, half:], up[:, half:]], axis=1)
    from_left = lax.ppermute(piece_b, "frame", shift(1))
    from_left_down = lax.ppermute(down[half:], "frame", shift(1))
    from_right = lax.ppermute(piece_a, "frame", shift(-1))
    from_right_down = lax.ppermute(down[:half], "frame", shift(-1))

    routing = jnp.concatenate(
        [route_experts[0].astype(jnp.float32), route_weights[0]], axis=1
    )
    routing = jnp.stack([routing, lax.ppermute(routing, "frame", shift(2))])
    routing = lax.all_gather(routing, "pixel", axis=1, tiled=True)

    spatial_packed = spatial_inputs.reshape(here, 3, HEADS, HDIM)
    spatial_all = lax.all_to_all(spatial_packed, "pixel", split_axis=2, concat_axis=0, tiled=True)
    spatial = attend(spatial_all[:, 0, 0], spatial_all[:, 1, 0], spatial_all[:, 2, 0])
    spatial = lax.all_to_all(spatial, "pixel", split_axis=0, concat_axis=1, tiled=True)

    temporal_packed = temporal_inputs.reshape(here, 3, HEADS, HDIM)
    temporal_all = lax.all_to_all(temporal_packed, "frame", split_axis=2, concat_axis=0, tiled=True)
    place = jnp.arange(here * frames) % here
    temporal = attend(
        temporal_all[:, 0, 0], temporal_all[:, 1, 0], temporal_all[:, 2, 0],
        place[:, None] == place[None, :],
    )
    temporal = lax.all_to_all(temporal, "frame", split_axis=0, concat_axis=1, tiled=True)

    combined = (
        tokens[0].astype(jnp.float32)
        + gate_spatial * spatial.astype(jnp.float32)
        + gate_temporal * temporal.astype(jnp.float32)
    )
    attended = combined.astype(jnp.bfloat16)
    widened = attended.astype(jnp.float32)
    mean_square = jnp.mean(widened * widened, axis=-1, keepdims=True)
    expert_input = (widened * lax.rsqrt(mean_square + 1e-06) * norm_gain).astype(jnp.bfloat16)

    both = jnp.stack([expert_input, lax.ppermute(expert_input, "frame", shift(2))])
    gathered = lax.all_gather(both, "pixel", axis=1, tiled=True)
    gathered = gathered.reshape(2, columns, here, model_width)

    experts = routing[:, :, :TOP].reshape(2, columns, here, 1, TOP)
    weights = routing[:, :, TOP:].reshape(2, columns, here, 1, TOP)
    mine = (
        lax.axis_index("pixel") * SIDE + jnp.arange(SIDE, dtype=jnp.int32)
    ).astype(jnp.float32)
    named = experts == mine[:, None]
    hit = jnp.any(named, axis=-1)
    weight = jnp.sum(jnp.where(named, weights, 0.0), axis=-1)
    rank = jnp.cumsum(hit.astype(jnp.int32), axis=2) - 1
    slots = jnp.arange(CAP, dtype=jnp.int32)
    chosen = hit[..., None] & (rank[..., None] == slots)
    select = chosen.astype(jnp.bfloat16)
    spread = jnp.where(chosen, weight[..., None], 0.0)

    rows = jnp.einsum(
        "fbtjr,fbtd->jfbrd", select, gathered, preferred_element_type=jnp.float32
    ).astype(jnp.bfloat16)
    groups = [[y * SIDE + x for y in range(SIDE)] for x in range(SIDE)]
    arrived = lax.all_to_all(
        rows, "frame", split_axis=0, concat_axis=0, tiled=True, axis_index_groups=groups
    )
    layout = arrived.shape
    flat = arrived.reshape(-1, model_width)

    def partial(gate_up, down_rows):
        width = down_rows.shape[0]
        both_halves = jnp.dot(flat, gate_up, preferred_element_type=jnp.float32)
        active = (jax.nn.silu(both_halves[:, :width]) * both_halves[:, width:]).astype(jnp.bfloat16)
        return jnp.dot(active, down_rows, preferred_element_type=jnp.float32)

    parts = (
        partial(expert_gate_up[0], down)
        + partial(from_left, from_left_down)
        + partial(from_right, from_right_down)
    )
    parts = parts.astype(jnp.bfloat16).reshape(layout)
    returned = lax.all_to_all(
        parts, "frame", split_axis=0, concat_axis=0, tiled=True, axis_index_groups=groups
    )
    mixed = jnp.einsum(
        "fbtjr,jfbrd->fbtd", spread.astype(jnp.bfloat16), returned,
        preferred_element_type=jnp.float32,
    ).astype(jnp.bfloat16).reshape(2, columns * here, model_width)
    mixed = lax.psum_scatter(mixed, "pixel", scatter_dimension=1, tiled=True)
    other = lax.ppermute(mixed[1], "frame", shift(2))
    expert_mix = (mixed[0].astype(jnp.float32) + other.astype(jnp.float32)).astype(jnp.bfloat16)
    return (attended[None], expert_mix[None])


def solution(mesh):
    in_specs = (
        P("frame", "pixel", None),
        P("frame", "pixel", None),
        P("frame", "pixel", None),
        P(),
        P(),
        P(),
        P("frame", "pixel", None),
        P("frame", "pixel", None),
        P(("frame", "pixel"), None, None),
        P(("frame", "pixel"), None, None),
    )
    out_specs = (P("frame", "pixel", None), P("frame", "pixel", None))
    return jax.shard_map(
        per_device, mesh=mesh, in_specs=in_specs, out_specs=out_specs, check_vma=False
    )
```

```python
import math

import jax
import jax.numpy as jnp
from jax import lax
from jax.experimental import pallas as pl
from jax.experimental.pallas import tpu as pltpu
from jax.sharding import PartitionSpec as P

BF16, F32 = jnp.bfloat16, jnp.float32
D = 2048
HEADS = 16
HDIM = 128
TOP = 6
CAP = 8
SIDE = 4
DEPTH = 8
HERE = 32
FF = 352
HALF = FF // 2
FF_PAD = 384
GROUP = 8 * HERE
SLOTS = GROUP // HERE * CAP
CHUNK = 512


def dot(a, b, dims=(1, 0)):
    return lax.dot_general(
        a, b, (((dims[0],), (dims[1],)), ((), ())), preferred_element_type=F32
    )


def iota(shape, axis):
    return lax.broadcasted_iota(jnp.int32, shape, axis)


def send(src, dst, send_sem, recv_sem, **where):
    pltpu.make_async_remote_copy(
        src_ref=src,
        dst_ref=dst,
        send_sem=send_sem,
        recv_sem=recv_sem,
        device_id=where,
        device_id_type=pl.DeviceIdType.MESH,
    ).start()


def wait_for(ref, sem):
    pltpu.make_async_copy(ref, ref, sem).wait()


def loop(low, high, body):
    def step(i, carry):
        body(i)
        return carry

    lax.fori_loop(low, high, step, 0)


def attend(packed, out, masked):
    def rows(i):
        queries = packed[0, pl.ds(4 * i, 4)].reshape(4 * HERE, HDIM)
        key_rows = packed[1].reshape(HEADS * HERE, HDIM)
        values = packed[2].reshape(HEADS * HERE, HDIM)
        scores = dot(queries, key_rows, (1, 1)) * (1.0 / math.sqrt(HDIM))
        if masked:
            same = iota(scores.shape, 0) % HERE == iota(scores.shape, 1) % HERE
            scores = jnp.where(same, scores, -1e30)
        weights = jnp.exp(scores - jnp.max(scores, axis=-1, keepdims=True))
        total = jnp.sum(weights, axis=-1, keepdims=True)
        result = dot(weights.astype(BF16), values) / total
        out[pl.ds(4 * i, 4)] = result.astype(BF16).reshape(4, HERE, HDIM)

    loop(0, 4, rows)


def kernel(
    tokens, spatial, temporal, gate_s, gate_t, gain, experts, weights, gate_up, down,
    attended_out, mix_out,
    own_gu, own_al, piece_a, piece_b, left_gu, right_gu, own_dn, left_dn, right_dn,
    s_out, s_in, t_out, t_in, s_part, t_part, s_ret, t_ret,
    r_out, r_in, rt, tok, sel, spr, rows_out, arrive, parts, back, mixed, sib, zred, zin,
    fin_out, fin_in,
    load_sem, w_send, w_recv, a_send, a_recv, r_send, r_recv, pair_send, pair_recv,
    z_send, z_recv, c_send, c_recv, y_send, y_recv, b_send, b_recv, m_send, m_recv,
    q_send, q_recv,
):
    f = lax.axis_index("frame")
    p = lax.axis_index("pixel")
    y, x = f // SIDE, f % SIDE
    z, c = p // 2, p % 2
    spot = z % 4

    def at_x(step):
        return y * SIDE + (x + step) % SIDE

    def at_y(other):
        return other * SIDE + x

    load_gu = pltpu.make_async_copy(gate_up, own_gu, load_sem.at[0])
    load_dn = pltpu.make_async_copy(down, own_dn.at[pl.ds(0, FF)], load_sem.at[1])
    load_gu.start()
    load_dn.start()

    barrier = pltpu.get_barrier_semaphore()

    def greet(i):
        pl.semaphore_signal(
            barrier, inc=1, device_id={"pixel": (p + i) % 16}, device_id_type=pl.DeviceIdType.MESH
        )
        pl.semaphore_signal(
            barrier, inc=1, device_id={"frame": (f + i) % 16}, device_id_type=pl.DeviceIdType.MESH
        )

    loop(1, 16, greet)

    for w in range(3):
        for h in range(HEADS):
            at = (w * HEADS + h) * HDIM
            s_out[w, h] = spatial[:, at : at + HDIM]
            t_out[w, h] = temporal[:, at : at + HDIM]
    place = (iota((HERE, 128), 1) == iota((HERE, 128), 0) + spot * HERE).astype(F32)
    exact = dict(precision=lax.Precision.HIGHEST, preferred_element_type=F32)
    over = (((0,), (0,)), ((), ()))
    r_out[...] = jnp.zeros_like(r_out)
    r_out[0:TOP] = lax.dot_general(experts[...].astype(F32), place, over, **exact)
    r_out[8 : 8 + TOP] = lax.dot_general(weights[...], place, over, **exact)

    pl.semaphore_wait(barrier, 30)

    def scatter_heads(i):
        to_f, to_p = (f + i) % 16, (p + i) % 16
        send(t_out.at[:, to_f], t_in.at[:, f], a_send.at[1], a_recv.at[1], frame=to_f)
        send(s_out.at[:, to_p], s_in.at[:, p], a_send.at[0], a_recv.at[0], pixel=to_p)

    loop(1, 16, scatter_heads)

    def scatter_routes(i):
        send(r_out, r_in.at[p], r_send.at[0], r_recv.at[0], pixel=(p + i) % 16)

    loop(1, 16, scatter_routes)
    s_in[:, p] = s_out[:, p]
    t_in[:, f] = t_out[:, f]
    r_in[p] = r_out[...]

    load_gu.wait()
    load_dn.wait()
    own_dn[FF:FF_PAD] = jnp.zeros((FF_PAD - FF, D), BF16)
    src, dst = iota((2 * FF, FF), 0), iota((2 * FF, FF), 1)
    pick_a = (src == jnp.where(dst < HALF, dst, dst + HALF)).astype(BF16)
    pick_b = (src == jnp.where(dst < HALF, dst + HALF, dst + 2 * HALF)).astype(BF16)
    src, dst = iota((2 * FF, 2 * FF_PAD), 0), iota((2 * FF, 2 * FF_PAD), 1)
    pick_al = (
        ((dst < FF) & (src == dst)) | ((dst >= FF_PAD) & (src == dst - FF_PAD + FF))
    ).astype(BF16)

    def cut(i):
        rows = pl.ds(i * 256, 256)
        block = own_gu[rows]
        piece_a[rows] = dot(block, pick_a).astype(BF16)
        piece_b[rows] = dot(block, pick_b).astype(BF16)

    loop(0, 8, cut)
    send(piece_a, right_gu, w_send.at[0], w_recv.at[0], frame=at_x(3))
    send(piece_b, left_gu, w_send.at[1], w_recv.at[1], frame=at_x(1))
    send(own_dn.at[pl.ds(0, HALF)], right_dn, w_send.at[2], w_recv.at[2], frame=at_x(3))
    send(own_dn.at[pl.ds(HALF, HALF)], left_dn, w_send.at[3], w_recv.at[3], frame=at_x(1))

    wait_for(t_in.at[:, pl.ds(0, 15)], a_recv.at[1])
    attend(t_in, t_part, True)

    def return_t(i):
        to = (f + i) % 16
        send(
            t_part.at[to], t_ret.at[:, pl.ds(pl.multiple_of(f * HDIM, HDIM), HDIM)],
            a_send.at[3], a_recv.at[3], frame=to,
        )

    loop(1, 16, return_t)
    t_ret[:, pl.ds(pl.multiple_of(f * HDIM, HDIM), HDIM)] = t_part[f]

    wait_for(s_in.at[:, pl.ds(0, 15)], a_recv.at[0])
    attend(s_in, s_part, False)

    def return_s(i):
        to = (p + i) % 16
        send(
            s_part.at[to], s_ret.at[:, pl.ds(pl.multiple_of(p * HDIM, HDIM), HDIM)],
            a_send.at[2], a_recv.at[2], pixel=to,
        )

    loop(1, 16, return_s)
    s_ret[:, pl.ds(pl.multiple_of(p * HDIM, HDIM), HDIM)] = s_part[p]

    wait_for(r_in.at[pl.ds(0, 15)], r_recv.at[0])
    for g in range(2):
        for core in range(2):
            total = None
            for q in range(4):
                block = r_in[(z + 7 + 4 * g + q) % DEPTH * 2 + core]
                total = block if total is None else total + block
            rt[0, g, core] = total
    send(rt.at[0], rt.at[1], r_send.at[1], r_recv.at[1], frame=at_x(2))

    def align(i):
        rows = pl.ds(i * 256, 256)
        own_al[rows] = dot(own_gu[rows], pick_al).astype(BF16)

    loop(0, 8, align)

    wait_for(t_ret.at[:, pl.ds(0, 15 * HDIM)], a_recv.at[3])
    wait_for(s_ret.at[:, pl.ds(0, 15 * HDIM)], a_recv.at[2])
    attended = (
        tokens[...].astype(F32)
        + gate_s[...] * s_ret[...].astype(F32)
        + gate_t[...] * t_ret[...].astype(F32)
    ).astype(BF16)
    attended_out[...] = attended
    widened = attended.astype(F32)
    mean_square = jnp.mean(widened * widened, axis=-1, keepdims=True)
    tok[0, 0, c, spot] = (widened * lax.rsqrt(mean_square + 1e-06) * gain[...]).astype(BF16)

    mine, other = tok.at[0, 0, c, spot], tok.at[1, 0, c, spot]
    send(mine, other, pair_send.at[0], pair_recv.at[0], frame=at_x(2))

    def spread_rows(frame, step):
        to = (z + step) % DEPTH
        group = (((DEPTH - step) + 1) % DEPTH) // 4
        send(
            tok.at[frame, 0, c, spot], tok.at[frame, group, c, spot],
            z_send.at[frame, step], z_recv.at[frame, group], pixel=to * 2 + c,
        )

    for step in (1, 7, 6):
        spread_rows(0, step)
    wait_for(other, pair_recv.at[0])
    for step in (1, 7, 6):
        spread_rows(1, step)
    for frame in range(2):
        for step in (5, 2, 3, 4):
            spread_rows(frame, step)
    wait_for(rt.at[1], r_recv.at[1])

    def dispatch(i):
        frame, g = i % 2, i // 2

        @pl.when(g == 0)
        def _():
            wait_for(tok.at[frame, 0, c, pl.ds(0, 3)], z_recv.at[frame, 0])

        @pl.when(g == 1)
        def _():
            wait_for(tok.at[frame, 1, c], z_recv.at[frame, 1])

        send(
            tok.at[frame, g, c], tok.at[frame, g, c],
            c_send.at[i], c_recv.at[i], pixel=z * 2 + 1 - c,
        )
        table = jnp.concatenate([rt[frame, g, 0], rt[frame, g, 1]], axis=1)
        hits, scales = [], []
        for j in range(SIDE):
            named = table[0:TOP] == (p * SIDE + j).astype(F32)
            hits.append(jnp.sum(named.astype(F32), axis=0, keepdims=True))
            scales.append(
                jnp.sum(jnp.where(named, table[8 : 8 + TOP], 0.0), axis=0, keepdims=True)
            )
        lanes = (GROUP, GROUP)
        before = (iota(lanes, 0) <= iota(lanes, 1)) & (
            iota(lanes, 0) // HERE == iota(lanes, 1) // HERE
        )
        hit = jnp.concatenate(hits + hits, axis=0)
        rank = dot(hit.astype(BF16), before.astype(BF16))
        base = (iota((1, GROUP), 1) // HERE * CAP).astype(F32) - 1.0
        number = iota((SLOTS, GROUP), 0).astype(F32)
        chosen, scaled = [], []
        for j in range(SIDE):
            slot = jnp.where(hits[j] > 0.5, base + rank[j : j + 1], -1.0)
            match = number == slot
            chosen.append(jnp.where(match, 1.0, 0.0))
            scaled.append(jnp.where(match, scales[j], 0.0))
        sel[...] = jnp.concatenate(chosen, axis=0).astype(BF16)
        spr[i] = jnp.transpose(jnp.concatenate(scaled, axis=0)).astype(BF16)
        wait_for(tok.at[frame, g, 1 - c], c_recv.at[i])

        def columns(n):
            at = pl.ds(pl.multiple_of(n * CHUNK, CHUNK), CHUNK)
            block = tok[frame, g, :, :, :, at].reshape(GROUP, CHUNK)
            rows_out[i, :, :, at] = (
                dot(sel[...], block).astype(BF16).reshape(SIDE, SLOTS, CHUNK)
            )

        loop(0, D // CHUNK, columns)
        for step in range(1, SIDE):
            to = (y + step) % SIDE
            send(
                rows_out.at[i, to], arrive.at[i, y], y_send.at[i], y_recv.at[i], frame=at_y(to)
            )
        arrive[i, y] = rows_out[i, y]

    def give_back(i):
        for step in range(1, SIDE):
            to = (y + step) % SIDE
            send(parts.at[i, to], back.at[i, y], b_send.at[i], b_recv.at[i], frame=at_y(to))

    def feed_forward(i):
        wait_for(arrive.at[i, pl.ds(0, SIDE - 1)], y_recv.at[i])
        flat = arrive[i].reshape(SIDE * SLOTS, D)

        def active(hidden, width, at):
            return (jax.nn.silu(hidden[:, :width]) * hidden[:, at : at + width]).astype(BF16)

        act_own = active(dot(flat, own_al[...]), FF_PAD, FF_PAD)
        act_left = active(dot(flat, left_gu[...]), HALF, HALF)
        act_right = active(dot(flat, right_gu[...]), HALF, HALF)

        def columns(n):
            at = pl.ds(pl.multiple_of(n * CHUNK, CHUNK), CHUNK)
            total = (
                dot(act_own, own_dn[:, at])
                + dot(act_left, left_dn[:, at])
                + dot(act_right, right_dn[:, at])
            )
            parts[i, :, :, at] = total.astype(BF16).reshape(SIDE, SLOTS, CHUNK)

        loop(0, D // CHUNK, columns)
        back[i, y] = parts[i, y]

        @pl.when(i >= 2)
        def _():
            give_back(i)

    def forward(k):
        @pl.when(k < 4)
        def _():
            dispatch(k)

        @pl.when(k == 2)
        def _():
            wait_for(left_gu, w_recv.at[1])
            wait_for(right_gu, w_recv.at[0])
            wait_for(left_dn, w_recv.at[3])
            wait_for(right_dn, w_recv.at[2])

        @pl.when(k >= 2)
        def _():
            feed_forward(k - 2)

    loop(0, 6, forward)
    give_back(1)
    give_back(0)

    def combine(k):
        i = jnp.where(k < 2, k + 2, 3 - k)
        frame, g = i % 2, i // 2
        wait_for(back.at[i, pl.ds(0, SIDE - 1)], b_recv.at[i])

        def columns(n):
            at = pl.ds(pl.multiple_of(n * CHUNK, CHUNK), CHUNK)
            block = back[i, :, :, at].reshape(SIDE * SLOTS, CHUNK)
            mixed[i, :, :, :, at] = (
                dot(spr[i], block).astype(BF16).reshape(2, 4, HERE, CHUNK)
            )

        loop(0, D // CHUNK, columns)
        send(mixed.at[i, 1 - c], sib.at[i], m_send.at[i], m_recv.at[i], pixel=z * 2 + 1 - c)
        wait_for(sib.at[i], m_recv.at[i])

        def blocks(q):
            zred[i, q] = (mixed[i, c, q].astype(F32) + sib[i, q].astype(F32)).astype(BF16)

        loop(0, 4, blocks)

        def out(step):
            to = (z + step) % DEPTH
            send(
                zred.at[i, to % 4], zin.at[frame, z], q_send.at[frame, step], q_recv.at[frame],
                pixel=to * 2 + c,
            )

        @pl.when(g == 0)
        def _():
            for step in (2, 7, 1):
                out(step)
            zin[frame, z] = zred[i, spot]

        @pl.when(g == 1)
        def _():
            for step in (4, 3, 5, 6):
                out(step)

    loop(0, 4, combine)

    def total(frame):
        wait_for(zin.at[frame, pl.ds(0, DEPTH - 1)], q_recv.at[frame])
        result = zin[frame, 0].astype(F32)
        for q in range(1, DEPTH):
            result = result + zin[frame, q].astype(F32)
        return result

    fin_out[...] = total(1).astype(BF16)
    send(fin_out, fin_in, pair_send.at[1], pair_recv.at[1], frame=at_x(2))
    own_total = total(0)
    wait_for(fin_in, pair_recv.at[1])
    mix_out[...] = (own_total + fin_in[...].astype(F32)).astype(BF16)

    wait_for(piece_a, w_send.at[0])
    wait_for(piece_b, w_send.at[1])
    wait_for(right_dn, w_send.at[2])
    wait_for(left_dn, w_send.at[3])
    wait_for(s_out.at[:, pl.ds(0, 15)], a_send.at[0])
    wait_for(t_out.at[:, pl.ds(0, 15)], a_send.at[1])
    wait_for(s_part.at[pl.ds(0, 15)], a_send.at[2])
    wait_for(t_part.at[pl.ds(0, 15)], a_send.at[3])
    wait_for(r_in.at[pl.ds(0, 15)], r_send.at[0])
    wait_for(rt.at[0], r_send.at[1])
    wait_for(mine, pair_send.at[0])
    wait_for(fin_out, pair_send.at[1])

    def sent(i):
        for frame in range(2):
            wait_for(tok.at[0, 0, 0, 0], z_send.at[frame, i])
            wait_for(zred.at[0, 0], q_send.at[frame, i])

    loop(1, DEPTH, sent)

    def sent_groups(i):
        wait_for(tok.at[0, 0, 0], c_send.at[i])
        wait_for(rows_out.at[i, pl.ds(0, SIDE - 1)], y_send.at[i])
        wait_for(parts.at[i, pl.ds(0, SIDE - 1)], b_send.at[i])
        wait_for(mixed.at[i, 0], m_send.at[i])

    loop(0, 4, sent_groups)


def per_device(
    tokens,
    spatial_inputs,
    temporal_inputs,
    gate_spatial,
    gate_temporal,
    norm_gain,
    route_experts,
    route_weights,
    expert_gate_up,
    expert_down,
):
    vmem = pl.BlockSpec(memory_space=pltpu.VMEM)
    hbm = pl.BlockSpec(memory_space=pl.ANY)
    dma = pltpu.SemaphoreType.DMA

    def buf(*shape, dtype=BF16):
        return pltpu.VMEM(shape, dtype)

    attended, mix = pl.pallas_call(
        kernel,
        out_shape=[jax.ShapeDtypeStruct((HERE, D), BF16)] * 2,
        in_specs=[vmem] * 8 + [hbm] * 2,
        out_specs=[vmem] * 2,
        scratch_shapes=[
            buf(D, 2 * FF), buf(D, 2 * FF_PAD), buf(D, FF), buf(D, FF), buf(D, FF), buf(D, FF),
            buf(FF_PAD, D), buf(HALF, D), buf(HALF, D),
            buf(3, HEADS, HERE, HDIM), buf(3, HEADS, HERE, HDIM),
            buf(3, HEADS, HERE, HDIM), buf(3, HEADS, HERE, HDIM),
            buf(HEADS, HERE, HDIM), buf(HEADS, HERE, HDIM), buf(HERE, D), buf(HERE, D),
            buf(16, 128, dtype=F32), buf(16, 16, 128, dtype=F32),
            buf(2, 2, 2, 16, 128, dtype=F32),
            buf(2, 2, 2, 4, HERE, D),
            buf(GROUP, GROUP), buf(4, GROUP, GROUP),
            buf(4, SIDE, SLOTS, D), buf(4, SIDE, SLOTS, D), buf(4, SIDE, SLOTS, D),
            buf(4, SIDE, SLOTS, D),
            buf(4, 2, 4, HERE, D), buf(4, 4, HERE, D), buf(4, 4, HERE, D),
            buf(2, DEPTH, HERE, D),
            buf(HERE, D), buf(HERE, D),
            dma((2,)), dma((4,)), dma((4,)), dma((4,)), dma((4,)), dma((2,)), dma((2,)),
            dma((2,)), dma((2,)), dma((2, DEPTH)), dma((2, 2)), dma((4,)), dma((4,)),
            dma((4,)), dma((4,)), dma((4,)), dma((4,)), dma((4,)), dma((4,)),
            dma((2, DEPTH)), dma((2,)),
        ],
        compiler_params=pltpu.CompilerParams(
            collective_id=0, has_side_effects=True, vmem_limit_bytes=60 * 1024 * 1024
        ),
    )(
        tokens[0],
        spatial_inputs[0],
        temporal_inputs[0],
        gate_spatial[None],
        gate_temporal[None],
        norm_gain[None],
        route_experts[0],
        route_weights[0],
        expert_gate_up[0],
        expert_down[0],
    )
    return (attended[None], mix[None])


def solution(mesh):
    in_specs = (
        P("frame", "pixel", None),
        P("frame", "pixel", None),
        P("frame", "pixel", None),
        P(),
        P(),
        P(),
        P("frame", "pixel", None),
        P("frame", "pixel", None),
        P(("frame", "pixel"), None, None),
        P(("frame", "pixel"), None, None),
    )
    out_specs = (P("frame", "pixel", None), P("frame", "pixel", None))
    return jax.shard_map(
        per_device, mesh=mesh, in_specs=in_specs, out_specs=out_specs, check_vma=False
    )
```

```python
import math

import jax
import jax.numpy as jnp
from jax import lax
from jax.experimental import pallas as pl
from jax.experimental.pallas import tpu as pltpu
from jax.sharding import PartitionSpec as P

BF16, F32 = jnp.bfloat16, jnp.float32
D = 2048
HEADS = 16
HDIM = 128
TOP = 6
CAP = 8
SIDE = 4
DEPTH = 8
HERE = 32
FF = 352
HALF = FF // 2
FF_PAD = 768
GROUP = 8 * HERE
SLOTS = GROUP // HERE * CAP
CHUNK = 512


def dot(a, b, dims=(1, 0)):
    return lax.dot_general(
        a, b, (((dims[0],), (dims[1],)), ((), ())), preferred_element_type=F32
    )


def iota(shape, axis):
    return lax.broadcasted_iota(jnp.int32, shape, axis)


def send(src, dst, send_sem, recv_sem, **where):
    pltpu.make_async_remote_copy(
        src_ref=src,
        dst_ref=dst,
        send_sem=send_sem,
        recv_sem=recv_sem,
        device_id=where,
        device_id_type=pl.DeviceIdType.MESH,
    ).start()


def wait_for(ref, sem):
    pltpu.make_async_copy(ref, ref, sem).wait()


def loop(low, high, body):
    def step(i, carry):
        body(i)
        return carry

    lax.fori_loop(low, high, step, 0)


def attend(packed, out, masked):
    def rows(i):
        queries = packed[0, pl.ds(4 * i, 4)].reshape(4 * HERE, HDIM)
        key_rows = packed[1].reshape(HEADS * HERE, HDIM)
        values = packed[2].reshape(HEADS * HERE, HDIM)
        scores = dot(queries, key_rows, (1, 1)) * (1.0 / math.sqrt(HDIM))
        if masked:
            same = iota(scores.shape, 0) % HERE == iota(scores.shape, 1) % HERE
            scores = jnp.where(same, scores, -1e30)
        weights = jnp.exp(scores - jnp.max(scores, axis=-1, keepdims=True))
        total = jnp.sum(weights, axis=-1, keepdims=True)
        result = dot(weights.astype(BF16), values) / total
        out[pl.ds(4 * i, 4)] = result.astype(BF16).reshape(4, HERE, HDIM)

    loop(0, 4, rows)


def kernel(
    tokens, spatial, temporal, gate_s, gate_t, gain, experts, weights, gate_up, down,
    attended_out, mix_out,
    gu_all, dn_all, act,
    s_out, s_in, t_out, t_in, s_part, t_part, s_ret, t_ret,
    r_out, r_in, rt, tok, sel, spr, rows_out, arrive, parts, back, mixed, sib, zred, zin,
    fin_out, fin_in,
    load_sem, w_send, w_recv, a_send, a_recv, r_send, r_recv, pair_send, pair_recv,
    z_send, z_recv, c_send, c_recv, y_send, y_recv, b_send, b_recv, m_send, m_recv,
    q_send, q_recv,
):
    f = lax.axis_index("frame")
    p = lax.axis_index("pixel")
    y, x = f // SIDE, f % SIDE
    z, c = p // 2, p % 2
    spot = z % 4

    def at_x(step):
        return y * SIDE + (x + step) % SIDE

    def at_y(other):
        return other * SIDE + x

    loads = [
        pltpu.make_async_copy(gate_up.at[pl.ds(0, FF)], gu_all.at[pl.ds(0, FF)], load_sem.at[0]),
        pltpu.make_async_copy(
            gate_up.at[pl.ds(FF, FF)], gu_all.at[pl.ds(FF_PAD, FF)], load_sem.at[1]
        ),
        pltpu.make_async_copy(down, dn_all.at[pl.ds(0, FF)], load_sem.at[2]),
    ]
    for load in loads:
        load.start()

    barrier = pltpu.get_barrier_semaphore()

    def greet(i):
        pl.semaphore_signal(
            barrier, inc=1, device_id={"pixel": (p + i) % 16}, device_id_type=pl.DeviceIdType.MESH
        )
        pl.semaphore_signal(
            barrier, inc=1, device_id={"frame": (f + i) % 16}, device_id_type=pl.DeviceIdType.MESH
        )

    loop(1, 16, greet)

    for w in range(3):
        for h in range(HEADS):
            at = (w * HEADS + h) * HDIM
            s_out[w, h] = spatial[:, at : at + HDIM]
            t_out[w, h] = temporal[:, at : at + HDIM]
    place = (iota((HERE, 128), 1) == iota((HERE, 128), 0) + spot * HERE).astype(F32)
    exact = dict(precision=lax.Precision.HIGHEST, preferred_element_type=F32)
    over = (((1,), (0,)), ((), ()))
    r_out[...] = jnp.zeros_like(r_out)
    r_out[0:TOP] = lax.dot_general(experts[:, 0].astype(F32), place, over, **exact)
    r_out[8 : 8 + TOP] = lax.dot_general(weights[:, 0], place, over, **exact)

    pl.semaphore_wait(barrier, 30)

    def scatter_heads(i):
        to_f, to_p = (f + i) % 16, (p + i) % 16
        send(t_out.at[:, to_f], t_in.at[:, f], a_send.at[1], a_recv.at[1], frame=to_f)
        send(s_out.at[:, to_p], s_in.at[:, p], a_send.at[0], a_recv.at[0], pixel=to_p)

    loop(1, 16, scatter_heads)

    def scatter_routes(i):
        send(r_out, r_in.at[p], r_send.at[0], r_recv.at[0], pixel=(p + i) % 16)

    loop(1, 16, scatter_routes)
    s_in[:, p] = s_out[:, p]
    t_in[:, f] = t_out[:, f]
    r_in[p] = r_out[...]

    wait_for(t_in.at[:, pl.ds(0, 15)], a_recv.at[1])

    for side, to, first, last in ((0, at_x(3), 0, FF + HALF), (1, at_x(1), HALF, FF)):
        for part, (source, start, target, base) in enumerate((
            (gate_up, first, gu_all, 0), (gate_up, FF + first, gu_all, FF_PAD),
            (down, first, dn_all, 0),
        )):
            send(
                source.at[pl.ds(start, HALF)], target.at[pl.ds(base + last, HALF)],
                w_send.at[side, part], w_recv.at[side, part], frame=to,
            )
    attend(t_in, t_part, True)

    def return_t(i):
        to = (f + i) % 16
        send(
            t_part.at[to], t_ret.at[:, pl.ds(pl.multiple_of(f * HDIM, HDIM), HDIM)],
            a_send.at[3], a_recv.at[3], frame=to,
        )

    loop(1, 16, return_t)
    t_ret[:, pl.ds(pl.multiple_of(f * HDIM, HDIM), HDIM)] = t_part[f]

    wait_for(s_in.at[:, pl.ds(0, 15)], a_recv.at[0])
    attend(s_in, s_part, False)

    def return_s(i):
        to = (p + i) % 16
        send(
            s_part.at[to], s_ret.at[:, pl.ds(pl.multiple_of(p * HDIM, HDIM), HDIM)],
            a_send.at[2], a_recv.at[2], pixel=to,
        )

    loop(1, 16, return_s)
    s_ret[:, pl.ds(pl.multiple_of(p * HDIM, HDIM), HDIM)] = s_part[p]

    wait_for(r_in.at[pl.ds(0, 15)], r_recv.at[0])
    for g in range(2):
        for core in range(2):
            total = None
            for q in range(4):
                block = r_in[(z + 7 + 4 * g + q) % DEPTH * 2 + core]
                total = block if total is None else total + block
            rt[0, g, core] = total
    send(rt.at[0], rt.at[1], r_send.at[1], r_recv.at[1], frame=at_x(2))

    for load in loads:
        load.wait()
    pad = 2 * FF
    gu_all[pad:FF_PAD] = jnp.zeros((FF_PAD - pad, D), BF16)
    gu_all[FF_PAD + pad :] = jnp.zeros((FF_PAD - pad, D), BF16)
    dn_all[pad:] = jnp.zeros((FF_PAD - pad, D), BF16)

    wait_for(t_ret.at[:, pl.ds(0, 15 * HDIM)], a_recv.at[3])
    wait_for(s_ret.at[:, pl.ds(0, 15 * HDIM)], a_recv.at[2])
    attended = (
        tokens[...].astype(F32)
        + gate_s[...] * s_ret[...].astype(F32)
        + gate_t[...] * t_ret[...].astype(F32)
    ).astype(BF16)
    attended_out[...] = attended
    widened = attended.astype(F32)
    mean_square = jnp.mean(widened * widened, axis=-1, keepdims=True)
    tok[0, 0, c, spot] = (widened * lax.rsqrt(mean_square + 1e-06) * gain[...]).astype(BF16)

    mine, other = tok.at[0, 0, c, spot], tok.at[1, 0, c, spot]
    send(mine, other, pair_send.at[0], pair_recv.at[0], frame=at_x(2))

    def spread_rows(frame, step):
        to = (z + step) % DEPTH
        group = (((DEPTH - step) + 1) % DEPTH) // 4
        send(
            tok.at[frame, 0, c, spot], tok.at[frame, group, c, spot],
            z_send.at[frame, step], z_recv.at[frame, group], pixel=to * 2 + c,
        )

    for step in (1, 7, 6):
        spread_rows(0, step)
    wait_for(other, pair_recv.at[0])
    for step in (1, 7, 6):
        spread_rows(1, step)
    for frame in range(2):
        for step in (5, 2, 3, 4):
            spread_rows(frame, step)
    wait_for(rt.at[1], r_recv.at[1])

    def dispatch(i):
        frame, g = i % 2, i // 2

        @pl.when(g == 0)
        def _():
            wait_for(tok.at[frame, 0, c, pl.ds(0, 3)], z_recv.at[frame, 0])

        @pl.when(g == 1)
        def _():
            wait_for(tok.at[frame, 1, c], z_recv.at[frame, 1])

        send(
            tok.at[frame, g, c], tok.at[frame, g, c],
            c_send.at[i], c_recv.at[i], pixel=z * 2 + 1 - c,
        )
        table = jnp.concatenate([rt[frame, g, 0], rt[frame, g, 1]], axis=1)
        hits, scales = [], []
        for j in range(SIDE):
            named = table[0:TOP] == (p * SIDE + j).astype(F32)
            hits.append(jnp.sum(named.astype(F32), axis=0, keepdims=True))
            scales.append(
                jnp.sum(jnp.where(named, table[8 : 8 + TOP], 0.0), axis=0, keepdims=True)
            )
        lanes = (GROUP, GROUP)
        before = (iota(lanes, 0) <= iota(lanes, 1)) & (
            iota(lanes, 0) // HERE == iota(lanes, 1) // HERE
        )
        hit = jnp.concatenate(hits + hits, axis=0)
        rank = dot(hit.astype(BF16), before.astype(BF16))
        base = (iota((1, GROUP), 1) // HERE * CAP).astype(F32) - 1.0
        number = iota((SLOTS, GROUP), 0).astype(F32)
        chosen, scaled = [], []
        for j in range(SIDE):
            slot = jnp.where(hits[j] > 0.5, base + rank[j : j + 1], -1.0)
            match = number == slot
            chosen.append(jnp.where(match, 1.0, 0.0))
            scaled.append(jnp.where(match, scales[j], 0.0))
        sel[...] = jnp.concatenate(chosen, axis=0).astype(BF16)
        spr[i] = jnp.transpose(jnp.concatenate(scaled, axis=0)).astype(BF16)
        wait_for(tok.at[frame, g, 1 - c], c_recv.at[i])

        def columns(n):
            at = pl.ds(pl.multiple_of(n * CHUNK, CHUNK), CHUNK)
            block = tok[frame, g, :, :, :, at].reshape(GROUP, CHUNK)
            rows_out[i, :, :, at] = (
                dot(sel[...], block).astype(BF16).reshape(SIDE, SLOTS, CHUNK)
            )

        loop(0, D // CHUNK, columns)
        for step in range(1, SIDE):
            to = (y + step) % SIDE
            send(
                rows_out.at[i, to], arrive.at[i, y], y_send.at[i], y_recv.at[i], frame=at_y(to)
            )
        arrive[i, y] = rows_out[i, y]

    def give_back(i):
        for step in range(1, SIDE):
            to = (y + step) % SIDE
            send(parts.at[i, to], back.at[i, y], b_send.at[i], b_recv.at[i], frame=at_y(to))

    def feed_forward(i):
        wait_for(arrive.at[i, pl.ds(0, SIDE - 1)], y_recv.at[i])
        flat = arrive[i].reshape(SIDE * SLOTS, D)

        def hidden(n):
            gate = dot(flat, gu_all[pl.ds(n * GROUP, GROUP)], (1, 1))
            up = dot(flat, gu_all[pl.ds(FF_PAD + n * GROUP, GROUP)], (1, 1))
            act[n] = (jax.nn.silu(gate) * up).astype(BF16)

        loop(0, FF_PAD // GROUP, hidden)

        def columns(n):
            at = pl.ds(pl.multiple_of(n * CHUNK, CHUNK), CHUNK)
            total = dot(act[0], dn_all[0:GROUP, at])
            for m in range(1, FF_PAD // GROUP):
                total = total + dot(act[m], dn_all[m * GROUP : (m + 1) * GROUP, at])
            parts[i, :, :, at] = total.astype(BF16).reshape(SIDE, SLOTS, CHUNK)

        loop(0, D // CHUNK, columns)
        back[i, y] = parts[i, y]

        @pl.when(i >= 2)
        def _():
            give_back(i)

    def forward(k):
        @pl.when(k < 4)
        def _():
            dispatch(k)

        @pl.when(k == 2)
        def _():
            for side in range(2):
                for part in range(3):
                    wait_for(dn_all.at[pl.ds(0, HALF)], w_recv.at[side, part])

        @pl.when(k >= 2)
        def _():
            feed_forward(k - 2)

    loop(0, 6, forward)
    give_back(1)
    give_back(0)

    def combine(k):
        i = jnp.where(k < 2, k + 2, 3 - k)
        frame, g = i % 2, i // 2
        wait_for(back.at[i, pl.ds(0, SIDE - 1)], b_recv.at[i])

        def columns(n):
            at = pl.ds(pl.multiple_of(n * CHUNK, CHUNK), CHUNK)
            block = back[i, :, :, at].reshape(SIDE * SLOTS, CHUNK)
            mixed[i, :, :, :, at] = (
                dot(spr[i], block).astype(BF16).reshape(2, 4, HERE, CHUNK)
            )

        loop(0, D // CHUNK, columns)
        send(mixed.at[i, 1 - c], sib.at[i], m_send.at[i], m_recv.at[i], pixel=z * 2 + 1 - c)
        wait_for(sib.at[i], m_recv.at[i])

        def blocks(q):
            zred[i, q] = (mixed[i, c, q].astype(F32) + sib[i, q].astype(F32)).astype(BF16)

        loop(0, 4, blocks)

        def out(step):
            to = (z + step) % DEPTH
            send(
                zred.at[i, to % 4], zin.at[frame, z], q_send.at[frame, step], q_recv.at[frame],
                pixel=to * 2 + c,
            )

        @pl.when(g == 0)
        def _():
            for step in (2, 7, 1):
                out(step)
            zin[frame, z] = zred[i, spot]

        @pl.when(g == 1)
        def _():
            for step in (4, 3, 5, 6):
                out(step)

    loop(0, 4, combine)

    def total(frame):
        wait_for(zin.at[frame, pl.ds(0, DEPTH - 1)], q_recv.at[frame])
        result = zin[frame, 0].astype(F32)
        for q in range(1, DEPTH):
            result = result + zin[frame, q].astype(F32)
        return result

    fin_out[...] = total(1).astype(BF16)
    send(fin_out, fin_in, pair_send.at[1], pair_recv.at[1], frame=at_x(2))
    own_total = total(0)
    wait_for(fin_in, pair_recv.at[1])
    mix_out[...] = (own_total + fin_in[...].astype(F32)).astype(BF16)

    for side in range(2):
        for part in range(3):
            wait_for(dn_all.at[pl.ds(0, HALF)], w_send.at[side, part])
    wait_for(s_out.at[:, pl.ds(0, 15)], a_send.at[0])
    wait_for(t_out.at[:, pl.ds(0, 15)], a_send.at[1])
    wait_for(s_part.at[pl.ds(0, 15)], a_send.at[2])
    wait_for(t_part.at[pl.ds(0, 15)], a_send.at[3])
    wait_for(r_in.at[pl.ds(0, 15)], r_send.at[0])
    wait_for(rt.at[0], r_send.at[1])
    wait_for(mine, pair_send.at[0])
    wait_for(fin_out, pair_send.at[1])

    def sent(i):
        for frame in range(2):
            wait_for(tok.at[0, 0, 0, 0], z_send.at[frame, i])
            wait_for(zred.at[0, 0], q_send.at[frame, i])

    loop(1, DEPTH, sent)

    def sent_groups(i):
        wait_for(tok.at[0, 0, 0], c_send.at[i])
        wait_for(rows_out.at[i, pl.ds(0, SIDE - 1)], y_send.at[i])
        wait_for(parts.at[i, pl.ds(0, SIDE - 1)], b_send.at[i])
        wait_for(mixed.at[i, 0], m_send.at[i])

    loop(0, 4, sent_groups)


def per_device(
    tokens,
    spatial_inputs,
    temporal_inputs,
    gate_spatial,
    gate_temporal,
    norm_gain,
    route_experts,
    route_weights,
    expert_gate_up,
    expert_down,
):
    vmem = pl.BlockSpec(memory_space=pltpu.VMEM)
    hbm = pl.BlockSpec(memory_space=pl.ANY)
    dma = pltpu.SemaphoreType.DMA

    def buf(*shape, dtype=BF16):
        return pltpu.VMEM(shape, dtype)

    attended, mix = pl.pallas_call(
        kernel,
        out_shape=[jax.ShapeDtypeStruct((HERE, D), BF16)] * 2,
        in_specs=[vmem] * 8 + [hbm] * 2,
        out_specs=[vmem] * 2,
        scratch_shapes=[
            buf(2 * FF_PAD, D), buf(FF_PAD, D), buf(FF_PAD // GROUP, GROUP, GROUP),
            buf(3, HEADS, HERE, HDIM), buf(3, HEADS, HERE, HDIM),
            buf(3, HEADS, HERE, HDIM), buf(3, HEADS, HERE, HDIM),
            buf(HEADS, HERE, HDIM), buf(HEADS, HERE, HDIM), buf(HERE, D), buf(HERE, D),
            buf(16, 128, dtype=F32), buf(16, 16, 128, dtype=F32),
            buf(2, 2, 2, 16, 128, dtype=F32),
            buf(2, 2, 2, 4, HERE, D),
            buf(GROUP, GROUP), buf(4, GROUP, GROUP),
            buf(4, SIDE, SLOTS, D), buf(4, SIDE, SLOTS, D), buf(4, SIDE, SLOTS, D),
            buf(4, SIDE, SLOTS, D),
            buf(4, 2, 4, HERE, D), buf(4, 4, HERE, D), buf(4, 4, HERE, D),
            buf(2, DEPTH, HERE, D),
            buf(HERE, D), buf(HERE, D),
            dma((3,)), dma((2, 3)), dma((2, 3)), dma((4,)), dma((4,)), dma((2,)), dma((2,)),
            dma((2,)), dma((2,)), dma((2, DEPTH)), dma((2, 2)), dma((4,)), dma((4,)),
            dma((4,)), dma((4,)), dma((4,)), dma((4,)), dma((4,)), dma((4,)),
            dma((2, DEPTH)), dma((2,)),
        ],
        compiler_params=pltpu.CompilerParams(
            collective_id=0, has_side_effects=True, vmem_limit_bytes=60 * 1024 * 1024
        ),
    )(
        tokens[0],
        spatial_inputs[0],
        temporal_inputs[0],
        gate_spatial[None],
        gate_temporal[None],
        norm_gain[None],
        jnp.transpose(route_experts, (2, 0, 1)),
        jnp.transpose(route_weights, (2, 0, 1)),
        jnp.transpose(expert_gate_up, (0, 2, 1))[0],
        expert_down[0],
    )
    return (attended[None], mix[None])


def solution(mesh):
    in_specs = (
        P("frame", "pixel", None),
        P("frame", "pixel", None),
        P("frame", "pixel", None),
        P(),
        P(),
        P(),
        P("frame", "pixel", None),
        P("frame", "pixel", None),
        P(("frame", "pixel"), None, None),
        P(("frame", "pixel"), None, None),
    )
    out_specs = (P("frame", "pixel", None), P("frame", "pixel", None))
    return jax.shard_map(
        per_device, mesh=mesh, in_specs=in_specs, out_specs=out_specs, check_vma=False
    )
```

```python
import math

import jax
import jax.numpy as jnp
from jax import lax
from jax.experimental import pallas as pl
from jax.experimental.pallas import tpu as pltpu
from jax.sharding import PartitionSpec as P

BF16, F32 = jnp.bfloat16, jnp.float32
D = 2048
HEADS = 16
HDIM = 128
TOP = 6
CAP = 8
SIDE = 4
DEPTH = 8
HERE = 32
FF = 352
HALF = FF // 2
FF_PAD = 768
GROUP = 8 * HERE
SLOTS = GROUP // HERE * CAP
CHUNK = 512


def dot(a, b, dims=(1, 0)):
    return lax.dot_general(
        a, b, (((dims[0],), (dims[1],)), ((), ())), preferred_element_type=F32
    )


def iota(shape, axis):
    return lax.broadcasted_iota(jnp.int32, shape, axis)


def send(src, dst, send_sem, recv_sem, **where):
    pltpu.make_async_remote_copy(
        src_ref=src,
        dst_ref=dst,
        send_sem=send_sem,
        recv_sem=recv_sem,
        device_id=where,
        device_id_type=pl.DeviceIdType.MESH,
    ).start()


def wait_for(ref, sem):
    pltpu.make_async_copy(ref, ref, sem).wait()


def loop(low, high, body):
    def step(i, carry):
        body(i)
        return carry

    lax.fori_loop(low, high, step, 0)


def attend(packed, out, masked):
    def rows(i):
        queries = packed[0, pl.ds(4 * i, 4)].reshape(4 * HERE, HDIM)
        key_rows = packed[1].reshape(HEADS * HERE, HDIM)
        values = packed[2].reshape(HEADS * HERE, HDIM)
        scores = dot(queries, key_rows, (1, 1)) * (1.0 / math.sqrt(HDIM))
        if masked:
            same = iota(scores.shape, 0) % HERE == iota(scores.shape, 1) % HERE
            scores = jnp.where(same, scores, -1e30)
        weights = jnp.exp(scores - jnp.max(scores, axis=-1, keepdims=True))
        total = jnp.sum(weights, axis=-1, keepdims=True)
        result = dot(weights.astype(BF16), values) / total
        out[pl.ds(4 * i, 4)] = result.astype(BF16).reshape(4, HERE, HDIM)

    loop(0, 4, rows)


def kernel(
    tokens, spatial, temporal, gate_s, gate_t, gain, experts, weights, gate_up, down,
    attended_out, mix_out,
    gu_all, dn_all, act,
    s_out, s_in, t_out, t_in, s_part, t_part, s_ret, t_ret,
    r_out, r_in, rt, tok, sel, spr, rows_out, arrive, parts, back, mixed, sib, zred, zin,
    zfar, fin_out, fin_in,
    load_sem, w_send, w_recv, a_send, a_recv, r_send, r_recv, pair_send, pair_recv,
    z_send, z_recv, c_send, c_recv, y_send, y_recv, b_send, b_recv, m_send, m_recv,
    q_send, q_recv,
):
    f = lax.axis_index("frame")
    p = lax.axis_index("pixel")
    y, x = f // SIDE, f % SIDE
    z, c = p // 2, p % 2
    spot = z % 4

    def at_x(step):
        return y * SIDE + (x + step) % SIDE

    def at_y(other):
        return other * SIDE + x

    loads = [
        pltpu.make_async_copy(gate_up.at[pl.ds(0, FF)], gu_all.at[pl.ds(0, FF)], load_sem.at[0]),
        pltpu.make_async_copy(
            gate_up.at[pl.ds(FF, FF)], gu_all.at[pl.ds(FF_PAD, FF)], load_sem.at[1]
        ),
        pltpu.make_async_copy(down, dn_all.at[pl.ds(0, FF)], load_sem.at[2]),
    ]
    for load in loads:
        load.start()

    barrier = pltpu.get_barrier_semaphore()

    def greet(i):
        pl.semaphore_signal(
            barrier, inc=1, device_id={"pixel": (p + i) % 16}, device_id_type=pl.DeviceIdType.MESH
        )
        pl.semaphore_signal(
            barrier, inc=1, device_id={"frame": (f + i) % 16}, device_id_type=pl.DeviceIdType.MESH
        )

    loop(1, 16, greet)

    for w in range(3):
        for h in range(HEADS):
            at = (w * HEADS + h) * HDIM
            s_out[w, h] = spatial[:, at : at + HDIM]
            t_out[w, h] = temporal[:, at : at + HDIM]
    place = (iota((HERE, 128), 1) == iota((HERE, 128), 0) + spot * HERE).astype(F32)
    exact = dict(precision=lax.Precision.HIGHEST, preferred_element_type=F32)
    over = (((1,), (0,)), ((), ()))
    r_out[...] = jnp.zeros_like(r_out)
    r_out[0:TOP] = lax.dot_general(experts[:, 0].astype(F32), place, over, **exact)
    r_out[8 : 8 + TOP] = lax.dot_general(weights[:, 0], place, over, **exact)

    pl.semaphore_wait(barrier, 30)

    def scatter_heads(i):
        to_f, to_p = (f + i) % 16, (p + i) % 16
        send(t_out.at[:, to_f], t_in.at[:, f], a_send.at[1], a_recv.at[1], frame=to_f)
        send(s_out.at[:, to_p], s_in.at[:, p], a_send.at[0], a_recv.at[0], pixel=to_p)

    loop(1, 16, scatter_heads)

    def scatter_routes(i):
        send(r_out, r_in.at[p], r_send.at[0], r_recv.at[0], pixel=(p + i) % 16)

    loop(1, 16, scatter_routes)
    s_in[:, p] = s_out[:, p]
    t_in[:, f] = t_out[:, f]
    r_in[p] = r_out[...]

    wait_for(t_in.at[:, pl.ds(0, 15)], a_recv.at[1])

    attend(t_in, t_part, True)

    def return_t(i):
        to = (f + i) % 16
        send(
            t_part.at[to], t_ret.at[:, pl.ds(pl.multiple_of(f * HDIM, HDIM), HDIM)],
            a_send.at[3], a_recv.at[3], frame=to,
        )

    loop(1, 16, return_t)
    t_ret[:, pl.ds(pl.multiple_of(f * HDIM, HDIM), HDIM)] = t_part[f]

    def share(part):
        source, start, target, base = (
            (gate_up, 0, gu_all, 0), (gate_up, FF, gu_all, FF_PAD), (down, 0, dn_all, 0)
        )[part]
        for side, to, first, last in ((0, at_x(3), 0, FF + HALF), (1, at_x(1), HALF, FF)):
            send(
                source.at[pl.ds(start + first, HALF)], target.at[pl.ds(base + last, HALF)],
                w_send.at[side, part], w_recv.at[side, part], frame=to,
            )

    share(0)

    wait_for(s_in.at[:, pl.ds(0, 15)], a_recv.at[0])
    attend(s_in, s_part, False)

    def return_s(i):
        to = (p + i) % 16
        send(
            s_part.at[to], s_ret.at[:, pl.ds(pl.multiple_of(p * HDIM, HDIM), HDIM)],
            a_send.at[2], a_recv.at[2], pixel=to,
        )

    loop(1, 16, return_s)
    s_ret[:, pl.ds(pl.multiple_of(p * HDIM, HDIM), HDIM)] = s_part[p]

    wait_for(r_in.at[pl.ds(0, 15)], r_recv.at[0])
    for g in range(2):
        for core in range(2):
            total = None
            for q in range(4):
                block = r_in[(z + 7 + 4 * g + q) % DEPTH * 2 + core]
                total = block if total is None else total + block
            rt[0, g, core] = total
    send(rt.at[0], rt.at[1], r_send.at[1], r_recv.at[1], frame=at_x(2))

    for load in loads:
        load.wait()
    pad = 2 * FF
    gu_all[pad:FF_PAD] = jnp.zeros((FF_PAD - pad, D), BF16)
    gu_all[FF_PAD + pad :] = jnp.zeros((FF_PAD - pad, D), BF16)
    dn_all[pad:] = jnp.zeros((FF_PAD - pad, D), BF16)

    wait_for(t_ret.at[:, pl.ds(0, 15 * HDIM)], a_recv.at[3])
    wait_for(s_ret.at[:, pl.ds(0, 15 * HDIM)], a_recv.at[2])
    attended = (
        tokens[...].astype(F32)
        + gate_s[...] * s_ret[...].astype(F32)
        + gate_t[...] * t_ret[...].astype(F32)
    ).astype(BF16)
    attended_out[...] = attended
    widened = attended.astype(F32)
    mean_square = jnp.mean(widened * widened, axis=-1, keepdims=True)
    tok[0, 0, c, spot] = (widened * lax.rsqrt(mean_square + 1e-06) * gain[...]).astype(BF16)

    mine, other = tok.at[0, 0, c, spot], tok.at[1, 0, c, spot]
    send(mine, other, pair_send.at[0], pair_recv.at[0], frame=at_x(2))

    def spread_near(frame):
        for step, way in ((7, 1), (1, 0), (6, 2)):
            at = spot
            send(
                tok.at[frame, 0, c, at], tok.at[frame, 0, c, at],
                z_send.at[frame, way], z_recv.at[frame, 0],
                pixel=(z + step) % DEPTH * 2 + c,
            )

    def spread_far(frame):
        for way, (block, step) in enumerate(((2, 7), (7, 1), (2, 6), (7, 2))):
            at = (z + block) % 4
            send(
                tok.at[frame, 0, c, at], tok.at[frame, 1, c, at],
                z_send.at[frame, 3 + way], z_recv.at[frame, 1],
                pixel=(z + step) % DEPTH * 2 + c,
            )

    spread_near(0)
    wait_for(other, pair_recv.at[0])
    spread_near(1)
    share(1)
    share(2)
    wait_for(rt.at[1], r_recv.at[1])

    def dispatch(i):
        frame, g = i % 2, i // 2

        @pl.when(g == 0)
        def _():
            wait_for(tok.at[frame, 0, c, pl.ds(0, 3)], z_recv.at[frame, 0])
            spread_far(frame)

        @pl.when(g == 1)
        def _():
            wait_for(tok.at[frame, 1, c], z_recv.at[frame, 1])

        send(
            tok.at[frame, g, c], tok.at[frame, g, c],
            c_send.at[i], c_recv.at[i], pixel=z * 2 + 1 - c,
        )
        table = jnp.concatenate([rt[frame, g, 0], rt[frame, g, 1]], axis=1)
        hits, scales = [], []
        for j in range(SIDE):
            named = table[0:TOP] == (p * SIDE + j).astype(F32)
            hits.append(jnp.sum(named.astype(F32), axis=0, keepdims=True))
            scales.append(
                jnp.sum(jnp.where(named, table[8 : 8 + TOP], 0.0), axis=0, keepdims=True)
            )
        lanes = (GROUP, GROUP)
        before = (iota(lanes, 0) <= iota(lanes, 1)) & (
            iota(lanes, 0) // HERE == iota(lanes, 1) // HERE
        )
        hit = jnp.concatenate(hits + hits, axis=0)
        rank = dot(hit.astype(BF16), before.astype(BF16))
        base = (iota((1, GROUP), 1) // HERE * CAP).astype(F32) - 1.0
        number = iota((SLOTS, GROUP), 0).astype(F32)
        chosen, scaled = [], []
        for j in range(SIDE):
            slot = jnp.where(hits[j] > 0.5, base + rank[j : j + 1], -1.0)
            match = number == slot
            chosen.append(jnp.where(match, 1.0, 0.0))
            scaled.append(jnp.where(match, scales[j], 0.0))
        sel[...] = jnp.concatenate(chosen, axis=0).astype(BF16)
        spr[i] = jnp.transpose(jnp.concatenate(scaled, axis=0)).astype(BF16)
        wait_for(tok.at[frame, g, 1 - c], c_recv.at[i])

        def columns(n):
            at = pl.ds(pl.multiple_of(n * CHUNK, CHUNK), CHUNK)
            block = tok[frame, g, :, :, :, at].reshape(GROUP, CHUNK)
            rows_out[i, :, :, at] = (
                dot(sel[...], block).astype(BF16).reshape(SIDE, SLOTS, CHUNK)
            )

        loop(0, D // CHUNK, columns)
        for step in range(1, SIDE):
            to = (y + step) % SIDE
            send(
                rows_out.at[i, to], arrive.at[i, y], y_send.at[i], y_recv.at[i], frame=at_y(to)
            )
        arrive[i, y] = rows_out[i, y]

    def give_back(i):
        for step in range(1, SIDE):
            to = (y + step) % SIDE
            send(parts.at[i, to], back.at[i, y], b_send.at[i], b_recv.at[i], frame=at_y(to))

    def feed_forward(i):
        wait_for(arrive.at[i, pl.ds(0, SIDE - 1)], y_recv.at[i])
        flat = arrive[i].reshape(SIDE * SLOTS, D)

        def hidden(n):
            gate = dot(flat, gu_all[pl.ds(n * GROUP, GROUP)], (1, 1))
            up = dot(flat, gu_all[pl.ds(FF_PAD + n * GROUP, GROUP)], (1, 1))
            act[n] = (jax.nn.silu(gate) * up).astype(BF16)

        loop(0, FF_PAD // GROUP, hidden)

        def columns(n):
            at = pl.ds(pl.multiple_of(n * CHUNK, CHUNK), CHUNK)
            total = dot(act[0], dn_all[0:GROUP, at])
            for m in range(1, FF_PAD // GROUP):
                total = total + dot(act[m], dn_all[m * GROUP : (m + 1) * GROUP, at])
            parts[i, :, :, at] = total.astype(BF16).reshape(SIDE, SLOTS, CHUNK)

        loop(0, D // CHUNK, columns)
        back[i, y] = parts[i, y]
        give_back(i)

    def order(k):
        return jnp.where(k < 2, k + 2, 3 - k)

    loop(0, 4, dispatch)
    for side in range(2):
        for part in range(3):
            wait_for(dn_all.at[pl.ds(0, HALF)], w_recv.at[side, part])
    loop(0, 4, lambda k: feed_forward(order(k)))

    def combine(k):
        i = order(k)
        frame, g = i % 2, i // 2
        wait_for(back.at[i, pl.ds(0, SIDE - 1)], b_recv.at[i])

        def columns(n):
            at = pl.ds(pl.multiple_of(n * CHUNK, CHUNK), CHUNK)
            block = back[i, :, :, at].reshape(SIDE * SLOTS, CHUNK)
            mixed[i, :, :, :, at] = (
                dot(spr[i], block).astype(BF16).reshape(2, 4, HERE, CHUNK)
            )

        loop(0, D // CHUNK, columns)
        send(mixed.at[i, 1 - c], sib.at[i], m_send.at[i], m_recv.at[i], pixel=z * 2 + 1 - c)
        wait_for(sib.at[i], m_recv.at[i])

        def put(q, value):
            zred[i, q] = value.astype(BF16)

        def summed(q):
            return mixed[i, c, q].astype(F32) + sib[i, q].astype(F32)

        def out(way, block, step, target):
            send(
                zred.at[i, (z + block) % 4], target, q_send.at[frame, way],
                q_recv.at[frame, g], pixel=(z + step) % DEPTH * 2 + c,
            )

        @pl.when(g == 1)
        def _():
            loop(0, 4, lambda q: put(q, summed(q)))
            out(3, 6, 7, zfar.at[frame, 0, 0])
            out(4, 3, 1, zfar.at[frame, 1, 0])
            out(5, 5, 6, zfar.at[frame, 0, 1])
            out(6, 4, 2, zfar.at[frame, 1, 1])

        @pl.when(g == 0)
        def _():
            wait_for(zfar.at[frame], q_recv.at[frame, 1])
            for side, block in ((1, 2), (0, 7)):
                q = (z + block) % 4
                far = zfar[frame, side, 0].astype(F32) + zfar[frame, side, 1].astype(F32)
                put(q, summed(q) + far)
            out(0, 2, 2, zin.at[frame, 0])
            out(1, 7, 7, zin.at[frame, 1])
            q = (z + 1) % 4
            put(q, summed(q))
            out(2, 1, 1, zin.at[frame, 2])
            zred[i, spot] = summed(spot).astype(BF16)

    loop(0, 4, combine)

    def total(frame):
        wait_for(zin.at[frame], q_recv.at[frame, 0])
        result = zred[frame, spot].astype(F32)
        for q in range(3):
            result = result + zin[frame, q].astype(F32)
        return result

    fin_out[...] = total(1).astype(BF16)
    send(fin_out, fin_in, pair_send.at[1], pair_recv.at[1], frame=at_x(2))
    own_total = total(0)
    wait_for(fin_in, pair_recv.at[1])
    mix_out[...] = (own_total + fin_in[...].astype(F32)).astype(BF16)

    for side in range(2):
        for part in range(3):
            wait_for(dn_all.at[pl.ds(0, HALF)], w_send.at[side, part])
    wait_for(s_out.at[:, pl.ds(0, 15)], a_send.at[0])
    wait_for(t_out.at[:, pl.ds(0, 15)], a_send.at[1])
    wait_for(s_part.at[pl.ds(0, 15)], a_send.at[2])
    wait_for(t_part.at[pl.ds(0, 15)], a_send.at[3])
    wait_for(r_in.at[pl.ds(0, 15)], r_send.at[0])
    wait_for(rt.at[0], r_send.at[1])
    wait_for(mine, pair_send.at[0])
    wait_for(fin_out, pair_send.at[1])

    def sent(i):
        for frame in range(2):
            wait_for(tok.at[0, 0, 0, 0], z_send.at[frame, i])
            wait_for(zred.at[0, 0], q_send.at[frame, i])

    loop(0, 7, sent)

    def sent_groups(i):
        wait_for(tok.at[0, 0, 0], c_send.at[i])
        wait_for(rows_out.at[i, pl.ds(0, SIDE - 1)], y_send.at[i])
        wait_for(parts.at[i, pl.ds(0, SIDE - 1)], b_send.at[i])
        wait_for(mixed.at[i, 0], m_send.at[i])

    loop(0, 4, sent_groups)


def per_device(
    tokens,
    spatial_inputs,
    temporal_inputs,
    gate_spatial,
    gate_temporal,
    norm_gain,
    route_experts,
    route_weights,
    expert_gate_up,
    expert_down,
):
    vmem = pl.BlockSpec(memory_space=pltpu.VMEM)
    hbm = pl.BlockSpec(memory_space=pl.ANY)
    dma = pltpu.SemaphoreType.DMA

    def buf(*shape, dtype=BF16):
        return pltpu.VMEM(shape, dtype)

    attended, mix = pl.pallas_call(
        kernel,
        out_shape=[jax.ShapeDtypeStruct((HERE, D), BF16)] * 2,
        in_specs=[vmem] * 8 + [hbm] * 2,
        out_specs=[vmem] * 2,
        scratch_shapes=[
            buf(2 * FF_PAD, D), buf(FF_PAD, D), buf(FF_PAD // GROUP, GROUP, GROUP),
            buf(3, HEADS, HERE, HDIM), buf(3, HEADS, HERE, HDIM),
            buf(3, HEADS, HERE, HDIM), buf(3, HEADS, HERE, HDIM),
            buf(HEADS, HERE, HDIM), buf(HEADS, HERE, HDIM), buf(HERE, D), buf(HERE, D),
            buf(16, 128, dtype=F32), buf(16, 16, 128, dtype=F32),
            buf(2, 2, 2, 16, 128, dtype=F32),
            buf(2, 2, 2, 4, HERE, D),
            buf(GROUP, GROUP), buf(4, GROUP, GROUP),
            buf(4, SIDE, SLOTS, D), buf(4, SIDE, SLOTS, D), buf(4, SIDE, SLOTS, D),
            buf(4, SIDE, SLOTS, D),
            buf(4, 2, 4, HERE, D), buf(4, 4, HERE, D), buf(4, 4, HERE, D),
            buf(2, 3, HERE, D), buf(2, 2, 2, HERE, D),
            buf(HERE, D), buf(HERE, D),
            dma((3,)), dma((2, 3)), dma((2, 3)), dma((4,)), dma((4,)), dma((2,)), dma((2,)),
            dma((2,)), dma((2,)), dma((2, 7)), dma((2, 2)), dma((4,)), dma((4,)),
            dma((4,)), dma((4,)), dma((4,)), dma((4,)), dma((4,)), dma((4,)),
            dma((2, 7)), dma((2, 2)),
        ],
        compiler_params=pltpu.CompilerParams(
            collective_id=0, has_side_effects=True, vmem_limit_bytes=60 * 1024 * 1024
        ),
    )(
        tokens[0],
        spatial_inputs[0],
        temporal_inputs[0],
        gate_spatial[None],
        gate_temporal[None],
        norm_gain[None],
        jnp.transpose(route_experts, (2, 0, 1)),
        jnp.transpose(route_weights, (2, 0, 1)),
        jnp.transpose(expert_gate_up, (0, 2, 1))[0],
        expert_down[0],
    )
    return (attended[None], mix[None])


def solution(mesh):
    in_specs = (
        P("frame", "pixel", None),
        P("frame", "pixel", None),
        P("frame", "pixel", None),
        P(),
        P(),
        P(),
        P("frame", "pixel", None),
        P("frame", "pixel", None),
        P(("frame", "pixel"), None, None),
        P(("frame", "pixel"), None, None),
    )
    out_specs = (P("frame", "pixel", None), P("frame", "pixel", None))
    return jax.shard_map(
        per_device, mesh=mesh, in_specs=in_specs, out_specs=out_specs, check_vma=False
    )
```

```python
import math

import jax
import jax.numpy as jnp
from jax import lax
from jax.experimental import pallas as pl
from jax.experimental.pallas import tpu as pltpu
from jax.sharding import PartitionSpec as P

BF16, F32 = jnp.bfloat16, jnp.float32
D = 2048
HEADS = 16
HDIM = 128
TOP = 6
CAP = 8
SIDE = 4
DEPTH = 8
HERE = 32
FF = 352
HALF = FF // 2
FF_PAD = 768
GROUP = 8 * HERE
SLOTS = GROUP // HERE * CAP
CHUNK = 512


def dot(a, b, dims=(1, 0)):
    return lax.dot_general(
        a, b, (((dims[0],), (dims[1],)), ((), ())), preferred_element_type=F32
    )


def iota(shape, axis):
    return lax.broadcasted_iota(jnp.int32, shape, axis)


def send(src, dst, send_sem, recv_sem, **where):
    pltpu.make_async_remote_copy(
        src_ref=src,
        dst_ref=dst,
        send_sem=send_sem,
        recv_sem=recv_sem,
        device_id=where,
        device_id_type=pl.DeviceIdType.MESH,
    ).start()


def wait_for(ref, sem):
    pltpu.make_async_copy(ref, ref, sem).wait()


def loop(low, high, body):
    def step(i, carry):
        body(i)
        return carry

    lax.fori_loop(low, high, step, 0)


def attend(packed, out, masked):
    def rows(i):
        queries = packed[0, pl.ds(4 * i, 4)].reshape(4 * HERE, HDIM)
        key_rows = packed[1].reshape(HEADS * HERE, HDIM)
        values = packed[2].reshape(HEADS * HERE, HDIM)
        scores = dot(queries, key_rows, (1, 1)) * (1.0 / math.sqrt(HDIM))
        if masked:
            same = iota(scores.shape, 0) % HERE == iota(scores.shape, 1) % HERE
            scores = jnp.where(same, scores, -1e30)
        weights = jnp.exp(scores - jnp.max(scores, axis=-1, keepdims=True))
        total = jnp.sum(weights, axis=-1, keepdims=True)
        result = dot(weights.astype(BF16), values) / total
        out[pl.ds(4 * i, 4)] = result.astype(BF16).reshape(4, HERE, HDIM)

    loop(0, 4, rows)


def kernel(
    tokens_in, spatial_in, temporal_in, gate_s, gate_t, gain, experts, weights, gate_up, down,
    attended_out, mix_out,
    tokens, spatial, temporal, gu_all, dn_all, act,
    s_out, s_in, t_out, t_in, s_part, t_part, s_ret, t_ret,
    r_out, r_in, rt, tok, sel, spr, rows_out, arrive, parts, back, mixed, sib, zred, zin,
    zfar, fin_out, fin_in, xin,
    load_sem, w_send, w_recv, a_send, a_recv, r_send, r_recv, pair_send, pair_recv,
    z_send, z_recv, c_send, c_recv, y_send, y_recv, b_send, b_recv, m_send, m_recv,
    q_send, q_recv, l_send, l_recv, nb_send, nb_recv, nm_send, nm_recv, nq_send, nq_recv,
):
    f = lax.axis_index("frame")
    p = lax.axis_index("pixel")
    y, x = f // SIDE, f % SIDE
    z, c = p // 2, p % 2
    spot = z % 4

    def at_x(step):
        return y * SIDE + (x + step) % SIDE

    def at_y(other):
        return other * SIDE + x

    barrier = pltpu.get_barrier_semaphore()

    def greet(i):
        pl.semaphore_signal(
            barrier, inc=1, device_id={"pixel": (p + i) % 16}, device_id_type=pl.DeviceIdType.MESH
        )
        pl.semaphore_signal(
            barrier, inc=1, device_id={"frame": (f + i) % 16}, device_id_type=pl.DeviceIdType.MESH
        )

    loop(1, 16, greet)

    loads = [
        pltpu.make_async_copy(source, target, load_sem.at[n])
        for n, (source, target) in enumerate((
            (spatial_in, spatial), (temporal_in, temporal), (tokens_in, tokens),
            (gate_up.at[pl.ds(0, FF)], gu_all.at[pl.ds(0, FF)]),
            (gate_up.at[pl.ds(FF, FF)], gu_all.at[pl.ds(FF_PAD, FF)]),
            (down, dn_all.at[pl.ds(0, FF)]),
        ))
    ]
    for load in loads:
        load.start()
    for load in loads[:2]:
        load.wait()
    for w in range(3):
        for h in range(HEADS):
            at = (w * HEADS + h) * HDIM
            s_out[w, h] = spatial[:, at : at + HDIM]
            t_out[w, h] = temporal[:, at : at + HDIM]
    place = (iota((HERE, 128), 1) == iota((HERE, 128), 0) + spot * HERE).astype(F32)
    exact = dict(precision=lax.Precision.HIGHEST, preferred_element_type=F32)
    over = (((1,), (0,)), ((), ()))
    blank = jnp.zeros((8 - TOP, 128), F32)
    r_out[...] = jnp.concatenate([
        lax.dot_general(experts[:, 0].astype(F32), place, over, **exact), blank,
        lax.dot_general(weights[:, 0], place, over, **exact), blank,
    ], axis=0).astype(BF16)

    pl.semaphore_wait(barrier, 30)

    def scatter_heads(i):
        to_f, to_p = (f + i) % 16, (p + i) % 16
        send(t_out.at[:, to_f], t_in.at[:, f], a_send.at[1], a_recv.at[1], frame=to_f)
        send(s_out.at[:, to_p], s_in.at[:, p], a_send.at[0], a_recv.at[0], pixel=to_p)

    loop(1, 16, scatter_heads)

    s_in[:, p] = s_out[:, p]
    t_in[:, f] = t_out[:, f]
    r_in[p] = r_out[...]

    shares = (
        (gate_up, 0, gu_all, 0, 0, 96), (gate_up, 0, gu_all, 0, 96, HALF - 96),
        (gate_up, FF, gu_all, FF_PAD, 0, HALF), (down, 0, dn_all, 0, 0, HALF),
    )

    def share(part):
        source, start, target, base, skip, count = shares[part]
        for side, to, first, last in ((0, at_x(3), 0, FF + HALF), (1, at_x(1), HALF, FF)):
            send(
                source.at[pl.ds(start + first + skip, count)],
                target.at[pl.ds(base + last + skip, count)],
                w_send.at[side, part], w_recv.at[side, part], frame=to,
            )

    share(0)

    wait_for(t_in.at[:, pl.ds(0, 15)], a_recv.at[1])

    attend(t_in, t_part, True)

    def return_t(i):
        to = (f + i) % 16
        send(
            t_part.at[to], t_ret.at[:, pl.ds(pl.multiple_of(f * HDIM, HDIM), HDIM)],
            a_send.at[3], a_recv.at[3], frame=to,
        )

    loop(1, 16, return_t)
    t_ret[:, pl.ds(pl.multiple_of(f * HDIM, HDIM), HDIM)] = t_part[f]

    share(1)
    wait_for(s_in.at[:, pl.ds(0, 15)], a_recv.at[0])

    def scatter_routes(i):
        send(r_out, r_in.at[p], r_send.at[0], r_recv.at[0], pixel=(p + i) % 16)

    loop(1, 16, scatter_routes)
    attend(s_in, s_part, False)

    def return_s(i):
        to = (p + i) % 16
        send(
            s_part.at[to], s_ret.at[:, pl.ds(pl.multiple_of(p * HDIM, HDIM), HDIM)],
            a_send.at[2], a_recv.at[2], pixel=to,
        )

    loop(1, 16, return_s)
    s_ret[:, pl.ds(pl.multiple_of(p * HDIM, HDIM), HDIM)] = s_part[p]

    wait_for(r_in.at[pl.ds(0, 15)], r_recv.at[0])
    for g in range(2):
        for core in range(2):
            total = None
            for q in range(4):
                block = r_in[(z + 7 + 4 * g + q) % DEPTH * 2 + core].astype(F32)
                total = block if total is None else total + block
            rt[0, g, core] = total.astype(BF16)
    send(rt.at[0], rt.at[1], r_send.at[1], r_recv.at[1], frame=at_x(2))

    for load in loads[2:]:
        load.wait()
    pad = 2 * FF
    gu_all[pad:FF_PAD] = jnp.zeros((FF_PAD - pad, D), BF16)
    gu_all[FF_PAD + pad :] = jnp.zeros((FF_PAD - pad, D), BF16)
    dn_all[pad:] = jnp.zeros((FF_PAD - pad, D), BF16)

    def build(i):
        frame, g = i % 2, i // 2
        table = jnp.concatenate([rt[frame, g, 0], rt[frame, g, 1]], axis=1).astype(F32)
        hits, scales = [], []
        for j in range(SIDE):
            named = table[0:TOP] == (p * SIDE + j).astype(F32)
            hits.append(jnp.sum(named.astype(F32), axis=0, keepdims=True))
            scales.append(
                jnp.sum(jnp.where(named, table[8 : 8 + TOP], 0.0), axis=0, keepdims=True)
            )
        lanes = (GROUP, GROUP)
        before = (iota(lanes, 0) <= iota(lanes, 1)) & (
            iota(lanes, 0) // HERE == iota(lanes, 1) // HERE
        )
        hit = jnp.concatenate(hits + hits, axis=0)
        rank = dot(hit.astype(BF16), before.astype(BF16))
        base = (iota((1, GROUP), 1) // HERE * CAP).astype(F32) - 1.0
        number = iota((SLOTS, GROUP), 0).astype(F32)
        chosen, scaled = [], []
        for j in range(SIDE):
            slot = jnp.where(hits[j] > 0.5, base + rank[j : j + 1], -1.0)
            match = number == slot
            chosen.append(jnp.where(match, 1.0, 0.0))
            scaled.append(jnp.where(match, scales[j], 0.0))
        sel[i] = jnp.concatenate(chosen, axis=0).astype(BF16)
        spr[i] = jnp.transpose(jnp.concatenate(scaled, axis=0)).astype(BF16)

    loop(0, 2, lambda g: build(2 * g))
    wait_for(t_ret.at[:, pl.ds(0, 15 * HDIM)], a_recv.at[3])
    wait_for(s_ret.at[:, pl.ds(0, 15 * HDIM)], a_recv.at[2])
    attended = (
        tokens[...].astype(F32)
        + gate_s[...] * s_ret[...].astype(F32)
        + gate_t[...] * t_ret[...].astype(F32)
    ).astype(BF16)
    attended_out[...] = attended
    widened = attended.astype(F32)
    mean_square = jnp.mean(widened * widened, axis=-1, keepdims=True)
    tok[0, 0, c, spot] = (widened * lax.rsqrt(mean_square + 1e-06) * gain[...]).astype(BF16)

    mine, other = tok.at[0, 0, c, spot], tok.at[1, 0, c, spot]
    send(mine, other, pair_send.at[0], pair_recv.at[0], frame=at_x(2))

    def pass_on(frame, block, step, group, way):
        at = (z + block) % 4
        send(
            tok.at[frame, 0, c, at], tok.at[frame, group, c, at],
            z_send.at[frame, way], z_recv.at[frame, min(way, 3)],
            pixel=(z + step) % DEPTH * 2 + c,
        )

    def wait_block(frame, way):
        wait_for(tok.at[frame, 0, c, 0], z_recv.at[frame, way])

    def start_near(frame):
        pass_on(frame, 0, 7, 0, 0)
        pass_on(frame, 0, 1, 0, 1)

    def second_near(frame):
        wait_block(frame, 0)
        pass_on(frame, 1, 7, 0, 2)

    def start_far(frame):
        for way, (block, step) in enumerate(((2, 7), (7, 1), (2, 6), (7, 2))):
            pass_on(frame, block, step, 1, 3 + way)

    def end_near(frame):
        wait_block(frame, 1)
        wait_block(frame, 2)
        to_sibling(frame, 0)

    def to_sibling(frame, g):
        send(
            tok.at[frame, g, c], tok.at[frame, g, c],
            c_send.at[frame, g], c_recv.at[frame, g], pixel=z * 2 + 1 - c,
        )

    def dispatch(frame, g):
        i = 2 * g + frame
        wait_for(tok.at[frame, g, 1 - c], c_recv.at[frame, g])

        def columns(n):
            at = pl.ds(pl.multiple_of(n * CHUNK, CHUNK), CHUNK)
            block = tok[frame, g, :, :, :, at].reshape(GROUP, CHUNK)
            rows_out[i, :, :, at] = (
                dot(sel[i], block).astype(BF16).reshape(SIDE, SLOTS, CHUNK)
            )

        loop(0, D // CHUNK, columns)
        for step in range(1, SIDE):
            to = (y + step) % SIDE
            send(
                rows_out.at[i, to], arrive.at[i, y], y_send.at[i], y_recv.at[i], frame=at_y(to)
            )
        arrive[i, y] = rows_out[i, y]

    start_near(0)
    second_near(0)
    wait_for(other, pair_recv.at[0])
    start_near(1)
    share(2)
    share(3)
    end_near(0)
    dispatch(0, 0)
    second_near(1)
    wait_for(rt.at[1], r_recv.at[1])
    loop(0, 2, lambda g: build(2 * g + 1))
    end_near(1)
    start_far(1)
    start_far(0)
    dispatch(1, 0)

    def dispatch_far(k):
        frame = 1 - k
        wait_for(tok.at[frame, 1, c], z_recv.at[frame, 3])
        to_sibling(frame, 1)
        dispatch(frame, 1)

    loop(0, 2, dispatch_far)

    def give_back(i):
        back[i, y] = parts[i, y]
        for step in range(1, SIDE):
            to = (y + step) % SIDE
            send(parts.at[i, to], back.at[i, y], b_send.at[i], b_recv.at[i], frame=at_y(to))

    def feed_forward(i):
        wait_for(arrive.at[i, pl.ds(0, SIDE - 1)], y_recv.at[i])
        flat = arrive[i].reshape(SIDE * SLOTS, D)

        def hidden(n):
            gate = dot(flat, gu_all[pl.ds(n * GROUP, GROUP)], (1, 1))
            up = dot(flat, gu_all[pl.ds(FF_PAD + n * GROUP, GROUP)], (1, 1))
            act[n] = (jax.nn.silu(gate) * up).astype(BF16)

        loop(0, FF_PAD // GROUP, hidden)

        def columns(n):
            at = pl.ds(pl.multiple_of(n * CHUNK, CHUNK), CHUNK)
            total = dot(act[0], dn_all[0:GROUP, at])
            for m in range(1, FF_PAD // GROUP):
                total = total + dot(act[m], dn_all[m * GROUP : (m + 1) * GROUP, at])
            parts[i, :, :, at] = total.astype(BF16).reshape(SIDE, SLOTS, CHUNK)

        loop(0, D // CHUNK, columns)

    for side in range(2):
        for part in range(4):
            wait_for(dn_all.at[pl.ds(0, shares[part][-1])], w_recv.at[side, part])

    def run_experts(k):
        i = jnp.where(k < 2, k, 5 - k)
        feed_forward(i)

        @pl.when(i == 1)
        def _():
            send(parts.at[1], xin, pair_send.at[2], pair_recv.at[2], frame=at_x(2))

        @pl.when(i >= 2)
        def _():
            give_back(i)

    loop(0, 4, run_experts)
    wait_for(xin, pair_recv.at[2])

    def chunk(n):
        return pl.ds(pl.multiple_of(n * CHUNK, CHUNK), CHUNK)

    def give_back_near(n):
        at = chunk(n)
        parts[0, :, :, at] = (
            parts[0, :, :, at].astype(F32) + xin[:, :, at].astype(F32)
        ).astype(BF16)
        back[0, y, :, at] = parts[0, y, :, at]
        for step in range(1, SIDE):
            to = (y + step) % SIDE
            send(
                parts.at[0, to, :, at], back.at[0, y, :, at],
                nb_send.at[n], nb_recv.at[n], frame=at_y(to),
            )

    loop(0, D // CHUNK, give_back_near)

    def combine(k):
        i = 3 - k
        frame = i % 2
        wait_for(back.at[i, pl.ds(0, SIDE - 1)], b_recv.at[i])

        def columns(n):
            at = chunk(n)
            block = back[i, :, :, at].reshape(SIDE * SLOTS, CHUNK)
            mixed[i, :, :, :, at] = (
                dot(spr[i], block).astype(BF16).reshape(2, 4, HERE, CHUNK)
            )

        loop(0, D // CHUNK, columns)
        send(mixed.at[i, 1 - c], sib.at[i], m_send.at[i], m_recv.at[i], pixel=z * 2 + 1 - c)
        wait_for(sib.at[i], m_recv.at[i])

        def put(q):
            zred[i, q] = (mixed[i, c, q].astype(F32) + sib[i, q].astype(F32)).astype(BF16)

        loop(0, 4, put)
        for way, (block, step, side, slot) in enumerate(
            ((6, 7, 0, 0), (3, 1, 1, 0), (5, 6, 0, 1), (4, 2, 1, 1))
        ):
            send(
                zred.at[i, (z + block) % 4], zfar.at[frame, side, slot], q_send.at[frame, way],
                q_recv.at[frame], pixel=(z + step) % DEPTH * 2 + c,
            )

    loop(0, 2, combine)
    wait_for(zfar.at[1], q_recv.at[1])
    for side, block in ((1, 2), (0, 7)):
        q = (z + block) % 4
        far = zfar[1, side, 0].astype(F32) + zfar[1, side, 1].astype(F32)
        zred[1, q] = far.astype(BF16)
        send(
            zred.at[1, q], zin.at[1, side], l_send.at[side], l_recv,
            pixel=(z + block) % DEPTH * 2 + c,
        )

    def combine_near(n):
        at = chunk(n)

        @pl.when(n == D // CHUNK - 1)
        def _():
            wait_for(zin.at[1, pl.ds(0, 2)], l_recv)
            fin_out[...] = (zin[1, 0].astype(F32) + zin[1, 1].astype(F32)).astype(BF16)
            send(fin_out, fin_in, pair_send.at[1], pair_recv.at[1], frame=at_x(2))

        wait_for(back.at[0, pl.ds(0, SIDE - 1), :, at], nb_recv.at[n])
        block = back[0, :, :, at].reshape(SIDE * SLOTS, CHUNK)
        mixed[0, :, :, :, at] = dot(spr[0], block).astype(BF16).reshape(2, 4, HERE, CHUNK)
        send(
            mixed.at[0, 1 - c, :, :, at], sib.at[0, :, :, at],
            nm_send.at[n], nm_recv.at[n], pixel=z * 2 + 1 - c,
        )
        wait_for(sib.at[0, :, :, at], nm_recv.at[n])

        @pl.when(n == 0)
        def _():
            wait_for(zfar.at[0], q_recv.at[0])

        for way, block in enumerate((2, 7, 1, 0)):
            q = (z + block) % 4
            total = mixed[0, c, q, :, at].astype(F32) + sib[0, q, :, at].astype(F32)
            if way < 2:
                for slot in range(2):
                    total = total + zfar[0, 1 - way, slot, :, at].astype(F32)
            zred[0, q, :, at] = total.astype(BF16)
            if way < 3:
                send(
                    zred.at[0, q, :, at], zin.at[0, way, :, at],
                    nq_send.at[way, n], nq_recv.at[n], pixel=(z + block) % DEPTH * 2 + c,
                )

    loop(0, D // CHUNK, combine_near)
    wait_for(fin_in, pair_recv.at[1])

    def finish(n):
        at = chunk(n)
        wait_for(zin.at[0, :, :, at], nq_recv.at[n])
        result = zred[0, spot, :, at].astype(F32) + fin_in[:, at].astype(F32)
        for way in range(3):
            result = result + zin[0, way, :, at].astype(F32)
        mix_out[:, at] = result.astype(BF16)

    loop(0, D // CHUNK, finish)

    for side in range(2):
        for part in range(4):
            wait_for(dn_all.at[pl.ds(0, shares[part][-1])], w_send.at[side, part])
    wait_for(s_out.at[:, pl.ds(0, 15)], a_send.at[0])
    wait_for(t_out.at[:, pl.ds(0, 15)], a_send.at[1])
    wait_for(s_part.at[pl.ds(0, 15)], a_send.at[2])
    wait_for(t_part.at[pl.ds(0, 15)], a_send.at[3])
    wait_for(r_in.at[pl.ds(0, 15)], r_send.at[0])
    wait_for(rt.at[0], r_send.at[1])
    wait_for(mine, pair_send.at[0])
    wait_for(fin_out, pair_send.at[1])

    def sent(i):
        for frame in range(2):
            wait_for(tok.at[0, 0, 0, 0], z_send.at[frame, i])

    loop(0, 7, sent)

    def sent_far(i):
        for frame in range(2):
            wait_for(zred.at[0, 0], q_send.at[frame, i])

    loop(0, 4, sent_far)
    for side in range(2):
        wait_for(zred.at[1, 0], l_send.at[side])
    wait_for(xin, pair_send.at[2])

    def sent_groups(i):
        wait_for(tok.at[0, 0, 0], c_send.at[i % 2, i // 2])
        wait_for(rows_out.at[i, pl.ds(0, SIDE - 1)], y_send.at[i])

        @pl.when(i >= 2)
        def _():
            wait_for(parts.at[i, pl.ds(0, SIDE - 1)], b_send.at[i])
            wait_for(mixed.at[i, 0], m_send.at[i])

    loop(0, 4, sent_groups)

    def sent_chunks(n):
        at = chunk(n)
        wait_for(parts.at[0, pl.ds(0, SIDE - 1), :, at], nb_send.at[n])
        wait_for(mixed.at[0, 0, :, :, at], nm_send.at[n])
        for way in range(3):
            wait_for(zred.at[0, 0, :, at], nq_send.at[way, n])

    loop(0, D // CHUNK, sent_chunks)


def per_device(
    tokens,
    spatial_inputs,
    temporal_inputs,
    gate_spatial,
    gate_temporal,
    norm_gain,
    route_experts,
    route_weights,
    expert_gate_up,
    expert_down,
):
    vmem = pl.BlockSpec(memory_space=pltpu.VMEM)
    hbm = pl.BlockSpec(memory_space=pl.ANY)
    dma = pltpu.SemaphoreType.DMA

    def buf(*shape, dtype=BF16):
        return pltpu.VMEM(shape, dtype)

    attended, mix = pl.pallas_call(
        kernel,
        out_shape=[jax.ShapeDtypeStruct((HERE, D), BF16)] * 2,
        in_specs=[hbm] * 3 + [vmem] * 5 + [hbm] * 2,
        out_specs=[vmem] * 2,
        scratch_shapes=[
            buf(HERE, D), buf(HERE, 3 * D), buf(HERE, 3 * D),
            buf(2 * FF_PAD, D), buf(FF_PAD, D), buf(FF_PAD // GROUP, GROUP, GROUP),
            buf(3, HEADS, HERE, HDIM), buf(3, HEADS, HERE, HDIM),
            buf(3, HEADS, HERE, HDIM), buf(3, HEADS, HERE, HDIM),
            buf(HEADS, HERE, HDIM), buf(HEADS, HERE, HDIM), buf(HERE, D), buf(HERE, D),
            buf(16, 128), buf(16, 16, 128), buf(2, 2, 2, 16, 128),
            buf(2, 2, 2, 4, HERE, D),
            buf(4, GROUP, GROUP), buf(4, GROUP, GROUP),
            buf(4, SIDE, SLOTS, D), buf(4, SIDE, SLOTS, D), buf(4, SIDE, SLOTS, D),
            buf(4, SIDE, SLOTS, D),
            buf(4, 2, 4, HERE, D), buf(4, 4, HERE, D), buf(4, 4, HERE, D),
            buf(2, 3, HERE, D), buf(2, 2, 2, HERE, D),
            buf(HERE, D), buf(HERE, D), buf(SIDE, SLOTS, D),
            dma((6,)), dma((2, 4)), dma((2, 4)), dma((4,)), dma((4,)), dma((2,)), dma((2,)),
            dma((3,)), dma((3,)), dma((2, 7)), dma((2, 4)), dma((2, 2)), dma((2, 2)),
            dma((4,)), dma((4,)), dma((4,)), dma((4,)), dma((4,)), dma((4,)),
            dma((2, 4)), dma((2,)), dma((2,)), dma(()), dma((4,)), dma((4,)), dma((4,)), dma((4,)),
            dma((3, 4)), dma((4,)),
        ],
        compiler_params=pltpu.CompilerParams(
            collective_id=0, has_side_effects=True, vmem_limit_bytes=60 * 1024 * 1024
        ),
    )(
        tokens[0],
        spatial_inputs[0],
        temporal_inputs[0],
        gate_spatial[None],
        gate_temporal[None],
        norm_gain[None],
        jnp.transpose(route_experts, (2, 0, 1)),
        jnp.transpose(route_weights, (2, 0, 1)),
        jnp.transpose(expert_gate_up, (0, 2, 1))[0],
        expert_down[0],
    )
    return (attended[None], mix[None])


def solution(mesh):
    in_specs = (
        P("frame", "pixel", None),
        P("frame", "pixel", None),
        P("frame", "pixel", None),
        P(),
        P(),
        P(),
        P("frame", "pixel", None),
        P("frame", "pixel", None),
        P(("frame", "pixel"), None, None),
        P(("frame", "pixel"), None, None),
    )
    out_specs = (P("frame", "pixel", None), P("frame", "pixel", None))
    return jax.shard_map(
        per_device, mesh=mesh, in_specs=in_specs, out_specs=out_specs, check_vma=False
    )
```

```python
import math

import jax
import jax.numpy as jnp
from jax import lax
from jax.experimental import pallas as pl
from jax.experimental.pallas import tpu as pltpu
from jax.sharding import PartitionSpec as P

BF16, F32 = jnp.bfloat16, jnp.float32
D = 2048
HEADS = 16
HDIM = 128
TOP = 6
CAP = 8
SIDE = 4
DEPTH = 8
HERE = 32
FF = 352
HALF = FF // 2
FF_PAD = 768
GROUP = 8 * HERE
SLOTS = GROUP // HERE * CAP
CHUNK = 512


def dot(a, b, dims=(1, 0)):
    return lax.dot_general(
        a, b, (((dims[0],), (dims[1],)), ((), ())), preferred_element_type=F32
    )


def iota(shape, axis):
    return lax.broadcasted_iota(jnp.int32, shape, axis)


def send(src, dst, send_sem, recv_sem, **where):
    pltpu.make_async_remote_copy(
        src_ref=src,
        dst_ref=dst,
        send_sem=send_sem,
        recv_sem=recv_sem,
        device_id=where,
        device_id_type=pl.DeviceIdType.MESH,
    ).start()


def wait_for(ref, sem):
    pltpu.make_async_copy(ref, ref, sem).wait()


def loop(low, high, body):
    def step(i, carry):
        body(i)
        return carry

    lax.fori_loop(low, high, step, 0)


def attend(packed, out, masked):
    def rows(i):
        queries = packed[0, pl.ds(4 * i, 4)].reshape(4 * HERE, HDIM)
        key_rows = packed[1].reshape(HEADS * HERE, HDIM)
        values = packed[2].reshape(HEADS * HERE, HDIM)
        scores = dot(queries, key_rows, (1, 1)) * (1.0 / math.sqrt(HDIM))
        if masked:
            same = iota(scores.shape, 0) % HERE == iota(scores.shape, 1) % HERE
            scores = jnp.where(same, scores, -1e30)
        weights = jnp.exp(scores - jnp.max(scores, axis=-1, keepdims=True))
        total = jnp.sum(weights, axis=-1, keepdims=True)
        result = dot(weights.astype(BF16), values) / total
        out[pl.ds(4 * i, 4)] = result.astype(BF16).reshape(4, HERE, HDIM)

    loop(0, 4, rows)


def kernel(
    tokens_in, spatial_in, temporal_in, gate_s, gate_t, gain, experts, weights, gate_up, down,
    out,
    tokens, spatial, temporal, gu_all, dn_all, act,
    s_out, s_in, t_out, t_in, s_part, t_part, s_ret, t_ret,
    r_out, r_in, rt, tok, sel, spr, rows_out, arrive, parts, back, mixed, sib, zred, zin,
    zfar, xfar, xin,
    load_sem, w_send, w_recv, a_send, a_recv, r_send, r_recv, pair_send, pair_recv,
    z_send, z_recv, c_send, c_recv, y_send, y_recv, b_send, b_recv, m_send, m_recv,
    q_send, q_recv, f_send, f_recv, nq_send, nq_recv,
):
    f = lax.axis_index("frame")
    p = lax.axis_index("pixel")
    y, x = f // SIDE, f % SIDE
    z, c = p // 2, p % 2
    spot = z % 4

    def at_x(step):
        return y * SIDE + (x + step) % SIDE

    def at_y(other):
        return other * SIDE + x

    barrier = pltpu.get_barrier_semaphore()

    def greet(i):
        pl.semaphore_signal(
            barrier, inc=1, device_id={"pixel": (p + i) % 16}, device_id_type=pl.DeviceIdType.MESH
        )
        pl.semaphore_signal(
            barrier, inc=1, device_id={"frame": (f + i) % 16}, device_id_type=pl.DeviceIdType.MESH
        )

    loop(1, 16, greet)

    loads = [
        pltpu.make_async_copy(source, target, load_sem.at[n])
        for n, (source, target) in enumerate((
            (spatial_in, spatial), (temporal_in, temporal), (tokens_in, tokens),
            (gate_up.at[pl.ds(0, FF)], gu_all.at[pl.ds(0, FF)]),
            (gate_up.at[pl.ds(FF, FF)], gu_all.at[pl.ds(FF_PAD, FF)]),
            (down, dn_all.at[pl.ds(0, FF)]),
        ))
    ]
    for load in loads:
        load.start()
    for load in loads[:2]:
        load.wait()
    for w in range(3):
        for h in range(HEADS):
            at = (w * HEADS + h) * HDIM
            s_out[w, h] = spatial[:, at : at + HDIM]
            t_out[w, h] = temporal[:, at : at + HDIM]
    place = (iota((HERE, 128), 1) == iota((HERE, 128), 0) + spot * HERE).astype(F32)
    exact = dict(precision=lax.Precision.HIGHEST, preferred_element_type=F32)
    over = (((1,), (0,)), ((), ()))
    blank = jnp.zeros((8 - TOP, 128), F32)
    r_out[...] = jnp.concatenate([
        lax.dot_general(experts[:, 0].astype(F32), place, over, **exact), blank,
        lax.dot_general(weights[:, 0], place, over, **exact), blank,
    ], axis=0).astype(BF16)

    pl.semaphore_wait(barrier, 30)

    def scatter_heads(i):
        to_f, to_p = (f + i) % 16, (p + i) % 16
        send(t_out.at[:, to_f], t_in.at[:, f], a_send.at[1], a_recv.at[1], frame=to_f)
        send(s_out.at[:, to_p], s_in.at[:, p], a_send.at[0], a_recv.at[0], pixel=to_p)

    loop(1, 16, scatter_heads)

    s_in[:, p] = s_out[:, p]
    t_in[:, f] = t_out[:, f]
    r_in[p] = r_out[...]

    shares = (
        (gate_up, 0, gu_all, 0, 0, 96), (gate_up, 0, gu_all, 0, 96, HALF - 96),
        (gate_up, FF, gu_all, FF_PAD, 0, HALF), (down, 0, dn_all, 0, 0, HALF),
    )

    def share(part):
        source, start, target, base, skip, count = shares[part]
        for side, to, first, last in ((0, at_x(3), 0, FF + HALF), (1, at_x(1), HALF, FF)):
            send(
                source.at[pl.ds(start + first + skip, count)],
                target.at[pl.ds(base + last + skip, count)],
                w_send.at[side, part], w_recv.at[side, part], frame=to,
            )

    share(0)

    wait_for(t_in.at[:, pl.ds(0, 15)], a_recv.at[1])


    attend(t_in, t_part, True)

    def return_t(i):
        to = (f + i) % 16
        send(
            t_part.at[to], t_ret.at[:, pl.ds(pl.multiple_of(f * HDIM, HDIM), HDIM)],
            a_send.at[3], a_recv.at[3], frame=to,
        )

    loop(1, 16, return_t)
    t_ret[:, pl.ds(pl.multiple_of(f * HDIM, HDIM), HDIM)] = t_part[f]

    share(1)
    wait_for(s_in.at[:, pl.ds(0, 15)], a_recv.at[0])

    def scatter_routes(i):
        send(r_out, r_in.at[p], r_send.at[0], r_recv.at[0], pixel=(p + i) % 16)

    loop(1, 16, scatter_routes)

    attend(s_in, s_part, False)

    def return_s(i):
        to = (p + i) % 16
        send(
            s_part.at[to], s_ret.at[:, pl.ds(pl.multiple_of(p * HDIM, HDIM), HDIM)],
            a_send.at[2], a_recv.at[2], pixel=to,
        )

    loop(1, 16, return_s)
    s_ret[:, pl.ds(pl.multiple_of(p * HDIM, HDIM), HDIM)] = s_part[p]

    wait_for(r_in.at[pl.ds(0, 15)], r_recv.at[0])
    for g in range(2):
        for core in range(2):
            total = None
            for q in range(4):
                block = r_in[(z + 7 + 4 * g + q) % DEPTH * 2 + core].astype(F32)
                total = block if total is None else total + block
            rt[0, g, core] = total.astype(BF16)
    send(rt.at[0], rt.at[1], r_send.at[1], r_recv.at[1], frame=at_x(2))

    for load in loads[2:]:
        load.wait()
    pad = 2 * FF
    gu_all[pad:FF_PAD] = jnp.zeros((FF_PAD - pad, D), BF16)
    gu_all[FF_PAD + pad :] = jnp.zeros((FF_PAD - pad, D), BF16)
    dn_all[pad:] = jnp.zeros((FF_PAD - pad, D), BF16)

    def build(i):
        frame, g = i % 2, i // 2
        table = jnp.concatenate([rt[frame, g, 0], rt[frame, g, 1]], axis=1).astype(F32)
        hits, scales = [], []
        for j in range(SIDE):
            named = table[0:TOP] == (p * SIDE + j).astype(F32)
            hits.append(jnp.sum(named.astype(F32), axis=0, keepdims=True))
            scales.append(
                jnp.sum(jnp.where(named, table[8 : 8 + TOP], 0.0), axis=0, keepdims=True)
            )
        lanes = (GROUP, GROUP)
        before = (iota(lanes, 0) <= iota(lanes, 1)) & (
            iota(lanes, 0) // HERE == iota(lanes, 1) // HERE
        )
        hit = jnp.concatenate(hits + hits, axis=0)
        rank = dot(hit.astype(BF16), before.astype(BF16))
        base = (iota((1, GROUP), 1) // HERE * CAP).astype(F32) - 1.0
        number = iota((SLOTS, GROUP), 0).astype(F32)
        chosen, scaled = [], []
        for j in range(SIDE):
            slot = jnp.where(hits[j] > 0.5, base + rank[j : j + 1], -1.0)
            match = number == slot
            chosen.append(jnp.where(match, 1.0, 0.0))
            scaled.append(jnp.where(match, scales[j], 0.0))
        sel[i] = jnp.concatenate(chosen, axis=0).astype(BF16)
        spr[i] = jnp.transpose(jnp.concatenate(scaled, axis=0)).astype(BF16)

    loop(0, 2, lambda g: build(2 * g))
    wait_for(t_ret.at[:, pl.ds(0, 15 * HDIM)], a_recv.at[3])
    wait_for(s_ret.at[:, pl.ds(0, 15 * HDIM)], a_recv.at[2])
    attended = (
        tokens[...].astype(F32)
        + gate_s[...] * s_ret[...].astype(F32)
        + gate_t[...] * t_ret[...].astype(F32)
    ).astype(BF16)
    out[0] = attended
    widened = attended.astype(F32)
    mean_square = jnp.mean(widened * widened, axis=-1, keepdims=True)
    tok[0, 0, c, spot] = (widened * lax.rsqrt(mean_square + 1e-06) * gain[...]).astype(BF16)

    mine, other = tok.at[0, 0, c, spot], tok.at[1, 0, c, spot]
    send(mine, other, pair_send.at[0], pair_recv.at[0], frame=at_x(2))

    def home(d):
        return 0 if -1 <= d <= 2 else 1

    def pass_on(frame, d, step):
        at, there = (z + d) % 4, d - step
        if there == -4:
            there = 4
        send(
            tok.at[frame, home(d), c, at], tok.at[frame, home(there), c, at],
            z_send.at[frame, there + 3], z_recv.at[frame, there + 3],
            pixel=(z + step) % DEPTH * 2 + c,
        )

    def got(frame, *blocks):
        for d in blocks:
            wait_for(tok.at[frame, home(d), c, 0], z_recv.at[frame, d + 3])

    def to_sibling(frame, g):
        send(
            tok.at[frame, g, c], tok.at[frame, g, c],
            c_send.at[frame, g], c_recv.at[frame, g], pixel=z * 2 + 1 - c,
        )

    def dispatch(frame, g):
        i = 2 * g + frame
        wait_for(tok.at[frame, g, 1 - c], c_recv.at[frame, g])

        def columns(n):
            at = pl.ds(pl.multiple_of(n * CHUNK, CHUNK), CHUNK)
            block = tok[frame, g, :, :, :, at].reshape(GROUP, CHUNK)
            rows_out[i, :, :, at] = (
                dot(sel[i], block).astype(BF16).reshape(SIDE, SLOTS, CHUNK)
            )

        for n in range(D // CHUNK):
            columns(n)
        for step in range(1, SIDE):
            to = (y + step) % SIDE
            send(
                rows_out.at[i, to], arrive.at[i, y], y_send.at[i], y_recv.at[i], frame=at_y(to)
            )
        arrive[i, y] = rows_out[i, y]

    pass_on(0, 0, -1)
    pass_on(0, 0, 1)
    got(0, 1, -1)
    pass_on(0, 1, -1)
    pass_on(0, -1, 1)
    wait_for(other, pair_recv.at[0])
    pass_on(1, 0, -1)
    pass_on(1, 0, 1)
    share(2)
    share(3)
    got(0, 2, -2)
    to_sibling(0, 0)
    pass_on(0, 2, -1)
    pass_on(0, -2, 1)
    got(1, 1, -1)
    pass_on(1, 1, -1)

    @pl.when(c == 1)
    def _():
        pass_on(1, -1, 1)

    dispatch(0, 0)
    got(0, 3, -3)
    pass_on(0, 3, -1)
    wait_for(rt.at[1], r_recv.at[1])
    loop(0, 2, lambda g: build(2 * g + 1))
    got(1, 2)
    to_sibling(1, 0)

    @pl.when(c == 1)
    def _():
        got(1, -2)
        pass_on(1, 2, -1)
        pass_on(1, -2, 1)

    got(0, 4)
    to_sibling(0, 1)
    dispatch(0, 1)

    @pl.when(c == 1)
    def _():
        got(1, 3, -3)
        pass_on(1, -3, 1)

    dispatch(1, 0)

    @pl.when(c == 1)
    def _():
        got(1, 4)
        to_sibling(1, 1)

    @pl.when(c == 0)
    def _():
        wait_for(tok.at[1, 1, 1], c_recv.at[1, 1])

    low, high = pl.ds(0, SLOTS // 2), pl.ds(SLOTS // 2, SLOTS // 2)
    chosen = sel[3, :, GROUP // 2 :].reshape(SIDE, SLOTS, GROUP // 2)[:, SLOTS // 2 :]
    chosen = chosen.reshape(SIDE * SLOTS // 2, GROUP // 2)
    for n in range(D // CHUNK):
        at = pl.ds(n * CHUNK, CHUNK)
        block = tok[1, 1, 1, :, :, at].reshape(GROUP // 2, CHUNK)
        rows_out[3, :, high, at] = (
            dot(chosen, block).astype(BF16).reshape(SIDE, SLOTS // 2, CHUNK)
        )
    for step in range(1, SIDE):
        to = (y + step) % SIDE
        send(
            rows_out.at[3, to, high], arrive.at[3, y, high], y_send.at[3], y_recv.at[3],
            frame=at_y(to),
        )
    arrive[3, y, high] = rows_out[3, y, high]
    wait_for(arrive.at[2, pl.ds(0, SIDE - 1)], y_recv.at[2])
    send(arrive.at[2, :, low], arrive.at[3, :, low], pair_send.at[3], pair_recv.at[3], frame=at_x(2))

    def chunk(n):
        return pl.ds(pl.multiple_of(n * CHUNK, CHUNK), CHUNK)

    def give_back(i, n):
        at = chunk(n)
        back[i, y, :, at] = parts[i, y, :, at]
        for step in range(1, SIDE):
            to = (y + step) % SIDE
            send(
                parts.at[i, to, :, at], back.at[i, y, :, at],
                b_send.at[i, n], b_recv.at[i, n], frame=at_y(to),
            )

    def feed_forward(i):
        flat = arrive[i].reshape(SIDE * SLOTS, D)

        def hidden(n):
            gate = dot(flat, gu_all[pl.ds(n * GROUP, GROUP)], (1, 1))
            up = dot(flat, gu_all[pl.ds(FF_PAD + n * GROUP, GROUP)], (1, 1))
            act[n] = (jax.nn.silu(gate) * up).astype(BF16)

        for n in range(FF_PAD // GROUP):
            hidden(n)

        def columns(n):
            at = pl.ds(pl.multiple_of(n * CHUNK, CHUNK), CHUNK)
            total = dot(act[0], dn_all[0:GROUP, at])
            for m in range(1, FF_PAD // GROUP):
                total = total + dot(act[m], dn_all[m * GROUP : (m + 1) * GROUP, at])
            parts[i, :, :, at] = total.astype(BF16).reshape(SIDE, SLOTS, CHUNK)

            @pl.when((i == 3) | ((i == 2) & (n < 2)))
            def _():
                give_back(i, n)

        for n in range(D // CHUNK):
            columns(n)

    for side in range(2):
        for part in range(4):
            wait_for(dn_all.at[pl.ds(0, shares[part][-1])], w_recv.at[side, part])

    def run_experts(k):
        i = k % 2 * 2 + k // 2

        @pl.when(i < 2)
        def _():
            wait_for(arrive.at[i, pl.ds(0, SIDE - 1)], y_recv.at[i])

        @pl.when(i == 3)
        def _():
            wait_for(arrive.at[3, pl.ds(0, SIDE - 1), high], y_recv.at[3])
            wait_for(arrive.at[3, :, low], pair_recv.at[3])

        feed_forward(i)

        @pl.when(i == 1)
        def _():
            send(parts.at[1], xin, pair_send.at[2], pair_recv.at[2], frame=at_x(2))

    loop(0, 4, run_experts)
    loop(2, 4, lambda n: give_back(2, n))
    def give_back_near(n):
        at = chunk(n)
        parts[0, :, :, at] = (
            parts[0, :, :, at].astype(F32) + xin[:, :, at].astype(F32)
        ).astype(BF16)
        give_back(0, n)

    def combine(i, n):
        at = chunk(n)
        wait_for(back.at[i, pl.ds(0, SIDE - 1), :, at], b_recv.at[i, n])
        block = back[i, :, :, at].reshape(SIDE * SLOTS, CHUNK)
        mixed[i, :, :, :, at] = dot(spr[i], block).astype(BF16).reshape(2, 4, HERE, CHUNK)
        send(
            mixed.at[i, 1 - c, :, :, at], sib.at[i, :, :, at],
            m_send.at[i, n], m_recv.at[i, n], pixel=z * 2 + 1 - c,
        )

    def summed(i, q, at):
        return mixed[i, c, q, :, at].astype(F32) + sib[i, q, :, at].astype(F32)

    def partner_far(n):
        at = chunk(n)
        combine(3, n)
        wait_for(sib.at[3, :, :, at], m_recv.at[3, n])
        for q in range(4):
            zred[3, q, :, at] = summed(3, q, at).astype(BF16)
        send(
            zred.at[3, :, :, at], xfar.at[:, :, at], f_send.at[n], f_recv.at[n], frame=at_x(2)
        )

    def own_far(n):
        at = chunk(n)
        wait_for(sib.at[2, :, :, at], m_recv.at[2, n])
        wait_for(xfar.at[:, :, at], f_recv.at[n])
        for way, (block, step, side, slot) in enumerate(
            ((5, 6, 0, 1), (4, 2, 1, 1), (6, 7, 0, 0), (3, 1, 1, 0))
        ):
            q = (z + block) % 4
            zred[2, q, :, at] = (summed(2, q, at) + xfar[q, :, at].astype(F32)).astype(BF16)
            send(
                zred.at[2, q, :, at], zfar.at[side, slot, :, at], q_send.at[way, n], q_recv.at[n],
                pixel=(z + step) % DEPTH * 2 + c,
            )

    def own_near(n):
        at = chunk(n)
        wait_for(sib.at[0, :, :, at], m_recv.at[0, n])
        wait_for(zfar.at[:, :, :, at], q_recv.at[n])
        for way, block in enumerate((2, 7, 1, 0)):
            q = (z + block) % 4
            total = summed(0, q, at)
            if way < 2:
                for slot in range(2):
                    total = total + zfar[1 - way, slot, :, at].astype(F32)
            zred[0, q, :, at] = total.astype(BF16)
            if way < 3:
                send(
                    zred.at[0, q, :, at], zin.at[way, :, at],
                    nq_send.at[way, n], nq_recv.at[n], pixel=(z + block) % DEPTH * 2 + c,
                )

    loop(0, 2, lambda n: combine(2, n))
    loop(0, 4, partner_far)
    wait_for(xin, pair_recv.at[2])
    loop(0, 4, give_back_near)
    loop(2, 4, lambda n: combine(2, n))

    loop(0, 3, own_far)

    for side in range(2):
        for part in range(4):
            wait_for(dn_all.at[pl.ds(0, shares[part][-1])], w_send.at[side, part])
    wait_for(s_out.at[:, pl.ds(0, 15)], a_send.at[0])
    wait_for(t_out.at[:, pl.ds(0, 15)], a_send.at[1])
    wait_for(s_part.at[pl.ds(0, 15)], a_send.at[2])
    wait_for(t_part.at[pl.ds(0, 15)], a_send.at[3])
    wait_for(r_in.at[pl.ds(0, 15)], r_send.at[0])
    wait_for(rt.at[0], r_send.at[1])
    wait_for(mine, pair_send.at[0])

    def sent(frame, *blocks):
        for d in blocks:
            wait_for(tok.at[0, 0, 0, 0], z_send.at[frame, d + 3])

    sent(0, -3, -2, -1, 1, 2, 3, 4)
    sent(1, -1, 1, 2)

    @pl.when(c == 1)
    def _():
        sent(1, -3, -2, 3, 4)
        wait_for(tok.at[0, 0, 0], c_send.at[1, 1])

    wait_for(xin, pair_send.at[2])

    def sent_groups(i):
        wait_for(tok.at[0, 0, 0], c_send.at[i % 2, i // 2])
        wait_for(rows_out.at[i, pl.ds(0, SIDE - 1)], y_send.at[i])

    loop(0, 3, sent_groups)
    wait_for(rows_out.at[3, pl.ds(0, SIDE - 1), high], y_send.at[3])
    wait_for(arrive.at[3, :, low], pair_send.at[3])

    def sent_parts(n):
        at = chunk(n)
        for i in (2, 3):
            wait_for(parts.at[i, pl.ds(0, SIDE - 1), :, at], b_send.at[i, n])

    loop(0, D // CHUNK, sent_parts)

    def last_steps(n):
        combine(0, n)
        own_near(n)

        @pl.when(n == 0)
        def _():
            own_far(3)

    loop(0, 4, last_steps)

    def finish(n):
        at = chunk(n)
        wait_for(zin.at[:, :, at], nq_recv.at[n])
        result = zred[0, spot, :, at].astype(F32)
        for way in range(3):
            result = result + zin[way, :, at].astype(F32)
        out[1, :, at] = result.astype(BF16)

    loop(0, 4, finish)

    def sent_chunks(n):
        at = chunk(n)
        for i in (0, 2, 3):
            wait_for(mixed.at[i, 0, :, :, at], m_send.at[i, n])
        wait_for(parts.at[0, pl.ds(0, SIDE - 1), :, at], b_send.at[0, n])
        for way in range(3):
            wait_for(zred.at[0, 0, :, at], nq_send.at[way, n])
        for way in range(4):
            wait_for(zred.at[0, 0, :, at], q_send.at[way, n])
        wait_for(zred.at[3, :, :, at], f_send.at[n])

    loop(0, D // CHUNK, sent_chunks)


def per_device(
    tokens,
    spatial_inputs,
    temporal_inputs,
    gate_spatial,
    gate_temporal,
    norm_gain,
    route_experts,
    route_weights,
    expert_gate_up,
    expert_down,
):
    vmem = pl.BlockSpec(memory_space=pltpu.VMEM)
    hbm = pl.BlockSpec(memory_space=pl.ANY)
    dma = pltpu.SemaphoreType.DMA

    def buf(*shape, dtype=BF16):
        return pltpu.VMEM(shape, dtype)

    both = pl.pallas_call(
        kernel,
        out_shape=jax.ShapeDtypeStruct((2, HERE, D), BF16),
        in_specs=[hbm] * 3 + [vmem] * 5 + [hbm] * 2,
        out_specs=vmem,
        scratch_shapes=[
            buf(HERE, D), buf(HERE, 3 * D), buf(HERE, 3 * D),
            buf(2 * FF_PAD, D), buf(FF_PAD, D), buf(FF_PAD // GROUP, GROUP, GROUP),
            buf(3, HEADS, HERE, HDIM), buf(3, HEADS, HERE, HDIM),
            buf(3, HEADS, HERE, HDIM), buf(3, HEADS, HERE, HDIM),
            buf(HEADS, HERE, HDIM), buf(HEADS, HERE, HDIM), buf(HERE, D), buf(HERE, D),
            buf(16, 128), buf(16, 16, 128), buf(2, 2, 2, 16, 128),
            buf(2, 2, 2, 4, HERE, D),
            buf(4, GROUP, GROUP), buf(4, GROUP, GROUP),
            buf(4, SIDE, SLOTS, D), buf(4, SIDE, SLOTS, D), buf(4, SIDE, SLOTS, D),
            buf(4, SIDE, SLOTS, D),
            buf(4, 2, 4, HERE, D), buf(4, 4, HERE, D), buf(4, 4, HERE, D),
            buf(3, HERE, D), buf(2, 2, HERE, D), buf(4, HERE, D),
            buf(SIDE, SLOTS, D),
            dma((6,)), dma((2, 4)), dma((2, 4)), dma((4,)), dma((4,)), dma((2,)), dma((2,)),
            dma((4,)), dma((4,)), dma((2, 8)), dma((2, 8)), dma((2, 2)), dma((2, 2)),
            dma((4,)), dma((4,)), dma((4, 4)), dma((4, 4)), dma((4, 4)), dma((4, 4)),
            dma((4, 4)), dma((4,)), dma((4,)), dma((4,)), dma((3, 4)), dma((4,)),
        ],
        compiler_params=pltpu.CompilerParams(
            collective_id=0, has_side_effects=True, vmem_limit_bytes=60 * 1024 * 1024
        ),
    )(
        tokens[0],
        spatial_inputs[0],
        temporal_inputs[0],
        gate_spatial[None],
        gate_temporal[None],
        norm_gain[None],
        jnp.transpose(route_experts, (2, 0, 1)),
        jnp.transpose(route_weights, (2, 0, 1)),
        jnp.transpose(expert_gate_up, (0, 2, 1))[0],
        expert_down[0],
    )
    return (both[:1], both[1:])


def solution(mesh):
    in_specs = (
        P("frame", "pixel", None),
        P("frame", "pixel", None),
        P("frame", "pixel", None),
        P(),
        P(),
        P(),
        P("frame", "pixel", None),
        P("frame", "pixel", None),
        P(("frame", "pixel"), None, None),
        P(("frame", "pixel"), None, None),
    )
    out_specs = (P("frame", "pixel", None), P("frame", "pixel", None))
    return jax.shard_map(
        per_device, mesh=mesh, in_specs=in_specs, out_specs=out_specs, check_vma=False
    )
```

```python
import math

import jax
import jax.numpy as jnp
from jax import lax
from jax.experimental import pallas as pl
from jax.experimental.pallas import tpu as pltpu
from jax.sharding import PartitionSpec as P

BF16, F32 = jnp.bfloat16, jnp.float32
D = 2048
HEADS = 16
HDIM = 128
TOP = 6
CAP = 8
SIDE = 4
DEPTH = 8
HERE = 32
FF = 352
HALF = FF // 2
FF_PAD = 768
GROUP = 8 * HERE
SLOTS = GROUP // HERE * CAP
CHUNK = 512


def dot(a, b, dims=(1, 0)):
    return lax.dot_general(
        a, b, (((dims[0],), (dims[1],)), ((), ())), preferred_element_type=F32
    )


def iota(shape, axis):
    return lax.broadcasted_iota(jnp.int32, shape, axis)


def send(src, dst, send_sem, recv_sem, **where):
    pltpu.make_async_remote_copy(
        src_ref=src,
        dst_ref=dst,
        send_sem=send_sem,
        recv_sem=recv_sem,
        device_id=where,
        device_id_type=pl.DeviceIdType.MESH,
    ).start()


def wait_for(ref, sem):
    pltpu.make_async_copy(ref, ref, sem).wait()


def loop(low, high, body):
    def step(i, carry):
        body(i)
        return carry

    lax.fori_loop(low, high, step, 0)


def attend(packed, out, masked):
    def rows(i):
        queries = packed[0, pl.ds(4 * i, 4)].reshape(4 * HERE, HDIM)
        key_rows = packed[1].reshape(HEADS * HERE, HDIM)
        values = packed[2].reshape(HEADS * HERE, HDIM)
        scores = dot(queries, key_rows, (1, 1)) * (1.0 / math.sqrt(HDIM))
        if masked:
            same = iota(scores.shape, 0) % HERE == iota(scores.shape, 1) % HERE
            scores = jnp.where(same, scores, -1e30)
        weights = jnp.exp(scores - jnp.max(scores, axis=-1, keepdims=True))
        total = jnp.sum(weights, axis=-1, keepdims=True)
        result = dot(weights.astype(BF16), values) / total
        out[pl.ds(4 * i, 4)] = result.astype(BF16).reshape(4, HERE, HDIM)

    loop(0, 4, rows)


def kernel(
    tokens_in, spatial_in, temporal_in, gate_s, gate_t, gain, experts, weights, gate_up, down,
    out,
    tokens, spatial, temporal, gu_all, dn_all, act,
    s_out, s_in, t_out, t_in, s_part, t_part, s_ret, t_ret,
    r_out, r_in, rt, tok, sel, spr, rows_out, arrive, parts, back, mixed, sib, zred, zin,
    zfar, xfar, xin,
    load_sem, w_send, w_recv, a_send, a_recv, r_send, r_recv, pair_send, pair_recv,
    z_send, z_recv, c_send, c_recv, y_send, y_recv, b_send, b_recv, m_send, m_recv,
    q_send, q_recv, f_send, f_recv, h_send, h_recv, nq_send, nq_recv,
):
    f = lax.axis_index("frame")
    p = lax.axis_index("pixel")
    y, x = f // SIDE, f % SIDE
    z, c = p // 2, p % 2
    spot = z % 4

    def at_x(step):
        return y * SIDE + (x + step) % SIDE

    def at_y(other):
        return other * SIDE + x

    barrier = pltpu.get_barrier_semaphore()

    def greet(i):
        pl.semaphore_signal(
            barrier, inc=1, device_id={"pixel": (p + i) % 16}, device_id_type=pl.DeviceIdType.MESH
        )
        pl.semaphore_signal(
            barrier, inc=1, device_id={"frame": (f + i) % 16}, device_id_type=pl.DeviceIdType.MESH
        )

    loop(1, 16, greet)

    loads = [
        pltpu.make_async_copy(source, target, load_sem.at[n])
        for n, (source, target) in enumerate((
            (spatial_in, spatial), (temporal_in, temporal), (tokens_in, tokens),
            (gate_up.at[pl.ds(0, FF)], gu_all.at[pl.ds(0, FF)]),
            (gate_up.at[pl.ds(FF, FF)], gu_all.at[pl.ds(FF_PAD, FF)]),
            (down, dn_all.at[pl.ds(0, FF)]),
        ))
    ]
    for load in loads:
        load.start()
    for load in loads[:2]:
        load.wait()
    for w in range(3):
        for h in range(HEADS):
            at = (w * HEADS + h) * HDIM
            s_out[w, h] = spatial[:, at : at + HDIM]
            t_out[w, h] = temporal[:, at : at + HDIM]
    place = (iota((HERE, 128), 1) == iota((HERE, 128), 0) + spot * HERE).astype(F32)
    exact = dict(precision=lax.Precision.HIGHEST, preferred_element_type=F32)
    over = (((1,), (0,)), ((), ()))
    blank = jnp.zeros((8 - TOP, 128), F32)
    r_out[...] = jnp.concatenate([
        lax.dot_general(experts[:, 0].astype(F32), place, over, **exact), blank,
        lax.dot_general(weights[:, 0], place, over, **exact), blank,
    ], axis=0).astype(BF16)

    pl.semaphore_wait(barrier, 30)

    def peer(k):
        return jnp.where(k % 2 == 1, 8 - k // 2, 8 + k // 2)

    def scatter_heads(k):
        to_f, to_p = (f + peer(k)) % 16, (p + peer(k)) % 16
        send(s_out.at[:, to_p], s_in.at[:, p], a_send.at[0], a_recv.at[0], pixel=to_p)
        send(t_out.at[:, to_f], t_in.at[:, f], a_send.at[1], a_recv.at[1], frame=to_f)

    loop(1, 16, scatter_heads)

    s_in[:, p] = s_out[:, p]
    t_in[:, f] = t_out[:, f]
    r_in[p] = r_out[...]

    shares = (
        (gate_up, 0, gu_all, 0, 0, 96), (gate_up, 0, gu_all, 0, 96, HALF - 96),
        (gate_up, FF, gu_all, FF_PAD, 0, HALF), (down, 0, dn_all, 0, 0, HALF),
    )

    def share(part):
        source, start, target, base, skip, count = shares[part]
        for side, to, first, last in ((0, at_x(3), 0, FF + HALF), (1, at_x(1), HALF, FF)):
            send(
                source.at[pl.ds(start + first + skip, count)],
                target.at[pl.ds(base + last + skip, count)],
                w_send.at[side, part], w_recv.at[side, part], frame=to,
            )

    share(0)

    wait_for(t_in.at[:, pl.ds(0, 15)], a_recv.at[1])


    attend(t_in, t_part, True)

    def return_t(i):
        to = (f + i) % 16
        send(
            t_part.at[to], t_ret.at[:, pl.ds(pl.multiple_of(f * HDIM, HDIM), HDIM)],
            a_send.at[3], a_recv.at[3], frame=to,
        )

    loop(1, 16, return_t)
    t_ret[:, pl.ds(pl.multiple_of(f * HDIM, HDIM), HDIM)] = t_part[f]

    share(1)
    wait_for(s_in.at[:, pl.ds(0, 15)], a_recv.at[0])

    def scatter_routes(i):
        send(r_out, r_in.at[p], r_send.at[0], r_recv.at[0], pixel=(p + i) % 16)

    loop(1, 16, scatter_routes)

    attend(s_in, s_part, False)

    def return_s(k):
        to = (p + peer(k)) % 16
        send(
            s_part.at[to], s_ret.at[:, pl.ds(pl.multiple_of(p * HDIM, HDIM), HDIM)],
            a_send.at[2], a_recv.at[2], pixel=to,
        )

    loop(1, 16, return_s)
    s_ret[:, pl.ds(pl.multiple_of(p * HDIM, HDIM), HDIM)] = s_part[p]

    wait_for(r_in.at[pl.ds(0, 15)], r_recv.at[0])
    for g in range(2):
        for core in range(2):
            total = None
            for q in range(4):
                block = r_in[(z + 7 + 4 * g + q) % DEPTH * 2 + core].astype(F32)
                total = block if total is None else total + block
            rt[0, g, core] = total.astype(BF16)
    send(rt.at[0], rt.at[1], r_send.at[1], r_recv.at[1], frame=at_x(2))

    for load in loads[2:]:
        load.wait()
    pad = 2 * FF
    gu_all[pad:FF_PAD] = jnp.zeros((FF_PAD - pad, D), BF16)
    gu_all[FF_PAD + pad :] = jnp.zeros((FF_PAD - pad, D), BF16)
    dn_all[pad:] = jnp.zeros((FF_PAD - pad, D), BF16)

    def build(i):
        frame, g = i % 2, i // 2
        table = jnp.concatenate([rt[frame, g, 0], rt[frame, g, 1]], axis=1).astype(F32)
        hits, scales = [], []
        for j in range(SIDE):
            named = table[0:TOP] == (p * SIDE + j).astype(F32)
            hits.append(jnp.sum(named.astype(F32), axis=0, keepdims=True))
            scales.append(
                jnp.sum(jnp.where(named, table[8 : 8 + TOP], 0.0), axis=0, keepdims=True)
            )
        lanes = (GROUP, GROUP)
        before = (iota(lanes, 0) <= iota(lanes, 1)) & (
            iota(lanes, 0) // HERE == iota(lanes, 1) // HERE
        )
        hit = jnp.concatenate(hits + hits, axis=0)
        rank = dot(hit.astype(BF16), before.astype(BF16))
        base = (iota((1, GROUP), 1) // HERE * CAP).astype(F32) - 1.0
        number = iota((SLOTS, GROUP), 0).astype(F32)
        chosen, scaled = [], []
        for j in range(SIDE):
            slot = jnp.where(hits[j] > 0.5, base + rank[j : j + 1], -1.0)
            match = number == slot
            chosen.append(jnp.where(match, 1.0, 0.0))
            scaled.append(jnp.where(match, scales[j], 0.0))
        sel[i] = jnp.concatenate(chosen, axis=0).astype(BF16)
        spr[i] = jnp.transpose(jnp.concatenate(scaled, axis=0)).astype(BF16)

    wait_for(t_ret.at[:, pl.ds(0, 15 * HDIM)], a_recv.at[3])
    wait_for(s_ret.at[:, pl.ds(0, 15 * HDIM)], a_recv.at[2])
    attended = (
        tokens[...].astype(F32)
        + gate_s[...] * s_ret[...].astype(F32)
        + gate_t[...] * t_ret[...].astype(F32)
    ).astype(BF16)
    out[0] = attended
    widened = attended.astype(F32)
    mean_square = jnp.mean(widened * widened, axis=-1, keepdims=True)
    tok[0, 0, c, spot] = (widened * lax.rsqrt(mean_square + 1e-06) * gain[...]).astype(BF16)

    mine, other = tok.at[0, 0, c, spot], tok.at[1, 0, c, spot]
    send(mine, other, pair_send.at[0], pair_recv.at[0], frame=at_x(2))

    def home(d):
        return 0 if -1 <= d <= 2 else 1

    def pass_on(frame, d, step):
        at, there = (z + d) % 4, d - step
        if there == -4:
            there = 4
        send(
            tok.at[frame, home(d), c, at], tok.at[frame, home(there), c, at],
            z_send.at[frame, there + 3], z_recv.at[frame, there + 3],
            pixel=(z + step) % DEPTH * 2 + c,
        )

    def got(frame, *blocks):
        for d in blocks:
            wait_for(tok.at[frame, home(d), c, 0], z_recv.at[frame, d + 3])

    def to_sibling(frame, g):
        send(
            tok.at[frame, g, c], tok.at[frame, g, c],
            c_send.at[frame, g], c_recv.at[frame, g], pixel=z * 2 + 1 - c,
        )

    def dispatch(frame, g):
        i = 2 * g + frame
        wait_for(tok.at[frame, g, 1 - c], c_recv.at[frame, g])

        def columns(n):
            at = pl.ds(pl.multiple_of(n * CHUNK, CHUNK), CHUNK)
            block = tok[frame, g, :, :, :, at].reshape(GROUP, CHUNK)
            rows_out[i, :, :, at] = (
                dot(sel[i], block).astype(BF16).reshape(SIDE, SLOTS, CHUNK)
            )

        for n in range(D // CHUNK):
            columns(n)
        for step in range(1, SIDE):
            to = (y + step) % SIDE
            send(
                rows_out.at[i, to], arrive.at[i, y], y_send.at[i], y_recv.at[i], frame=at_y(to)
            )
        arrive[i, y] = rows_out[i, y]

    pass_on(0, 0, -1)
    pass_on(0, 0, 1)
    pass_on(0, 0, -2)
    loop(0, 2, lambda g: build(2 * g))
    got(0, 1, -1)
    pass_on(0, -1, 1)
    wait_for(other, pair_recv.at[0])
    pass_on(1, 0, -1)
    pass_on(1, 0, 1)
    share(2)
    share(3)
    got(0, 2, -2)
    to_sibling(0, 0)
    pass_on(0, 2, -1)
    pass_on(0, -2, 1)
    got(1, 1, -1)
    pass_on(1, 1, -1)

    @pl.when(c == 1)
    def _():
        pass_on(1, -1, 1)

    dispatch(0, 0)
    got(0, 3, -3)
    pass_on(0, 3, -1)
    wait_for(rt.at[1], r_recv.at[1])
    loop(0, 2, lambda g: build(2 * g + 1))
    got(1, 2)
    to_sibling(1, 0)

    @pl.when(c == 1)
    def _():
        got(1, -2)
        pass_on(1, 2, -1)
        pass_on(1, -2, 1)

    got(0, 4)
    to_sibling(0, 1)
    dispatch(0, 1)

    @pl.when(c == 1)
    def _():
        got(1, 3, -3)
        pass_on(1, -3, 1)

    dispatch(1, 0)

    @pl.when(c == 1)
    def _():
        got(1, 4)
        to_sibling(1, 1)

    @pl.when(c == 0)
    def _():
        wait_for(tok.at[1, 1, 1], c_recv.at[1, 1])

    low, high = pl.ds(0, SLOTS // 2), pl.ds(SLOTS // 2, SLOTS // 2)
    chosen = sel[3, :, GROUP // 2 :].reshape(SIDE, SLOTS, GROUP // 2)[:, SLOTS // 2 :]
    chosen = chosen.reshape(SIDE * SLOTS // 2, GROUP // 2)
    for n in range(D // CHUNK):
        at = pl.ds(n * CHUNK, CHUNK)
        block = tok[1, 1, 1, :, :, at].reshape(GROUP // 2, CHUNK)
        rows_out[3, :, high, at] = (
            dot(chosen, block).astype(BF16).reshape(SIDE, SLOTS // 2, CHUNK)
        )
    for step in range(1, SIDE):
        to = (y + step) % SIDE
        send(
            rows_out.at[3, to, high], arrive.at[3, y, high], y_send.at[3], y_recv.at[3],
            frame=at_y(to),
        )
    arrive[3, y, high] = rows_out[3, y, high]
    wait_for(arrive.at[2, pl.ds(0, SIDE - 1)], y_recv.at[2])
    send(arrive.at[2, :, low], arrive.at[3, :, low], pair_send.at[3], pair_recv.at[3], frame=at_x(2))

    def chunk(n):
        return pl.ds(pl.multiple_of(n * CHUNK, CHUNK), CHUNK)

    def give_back(i, n):
        at = chunk(n)
        back[i, y, :, at] = parts[i, y, :, at]
        for step in (2, 1, 3):
            to = (y + step) % SIDE
            send(
                parts.at[i, to, :, at], back.at[i, y, :, at],
                b_send.at[i, n], b_recv.at[i, n], frame=at_y(to),
            )

    def feed_forward(i):
        flat = arrive[i].reshape(SIDE * SLOTS, D)

        def hidden(n):
            gate = dot(flat, gu_all[pl.ds(n * GROUP, GROUP)], (1, 1))
            up = dot(flat, gu_all[pl.ds(FF_PAD + n * GROUP, GROUP)], (1, 1))
            act[n] = (jax.nn.silu(gate) * up).astype(BF16)

        for n in range(FF_PAD // GROUP):
            hidden(n)

        def columns(n):
            at = pl.ds(pl.multiple_of(n * CHUNK, CHUNK), CHUNK)
            total = dot(act[0], dn_all[0:GROUP, at])
            for m in range(1, FF_PAD // GROUP):
                total = total + dot(act[m], dn_all[m * GROUP : (m + 1) * GROUP, at])
            parts[i, :, :, at] = total.astype(BF16).reshape(SIDE, SLOTS, CHUNK)

            @pl.when(i == 1)
            def _():
                send(
                    parts.at[1, :, :, at], xin.at[:, :, at], h_send.at[n], h_recv.at[n],
                    frame=at_x(2),
                )

            @pl.when(((i == 3) & (n < 1)) | ((i == 2) & (n < 2)))
            def _():
                give_back(i, n)

        for n in range(D // CHUNK):
            columns(n)

    for side in range(2):
        for part in range(4):
            wait_for(dn_all.at[pl.ds(0, shares[part][-1])], w_recv.at[side, part])

    def run_experts(k):
        i = k % 2 * 2 + k // 2

        @pl.when(i < 2)
        def _():
            wait_for(arrive.at[i, pl.ds(0, SIDE - 1)], y_recv.at[i])

        @pl.when(i == 3)
        def _():
            wait_for(arrive.at[3, pl.ds(0, SIDE - 1), high], y_recv.at[3])
            wait_for(arrive.at[3, :, low], pair_recv.at[3])

        feed_forward(i)


    loop(0, 4, run_experts)
    def issue(k):
        late = (k >= 2) & (k < 6)
        i = jnp.where(late, 3, jnp.where(k < 8, 2, 0))
        n = jnp.where(late, k - 2, jnp.where(k < 2, k, jnp.where(k < 8, k - 4, k - 8)))
        at = chunk(n)

        @pl.when((k >= 8) & (k < 12))
        def _():
            wait_for(xin.at[:, :, at], h_recv.at[n])
            parts[0, :, :, at] = (
                parts[0, :, :, at].astype(F32) + xin[:, :, at].astype(F32)
            ).astype(BF16)

        @pl.when(k < 12)
        def _():
            give_back(i, n)

    def combine(i, n):
        at = chunk(n)
        wait_for(back.at[i, pl.ds(0, SIDE - 1), :, at], b_recv.at[i, n])
        block = back[i, :, :, at].reshape(SIDE * SLOTS, CHUNK)
        mixed[i, :, :, :, at] = dot(spr[i], block).astype(BF16).reshape(2, 4, HERE, CHUNK)
        send(
            mixed.at[i, 1 - c, :, :, at], sib.at[i, :, :, at],
            m_send.at[i, n], m_recv.at[i, n], pixel=z * 2 + 1 - c,
        )

    def summed(i, q, at):
        return mixed[i, c, q, :, at].astype(F32) + sib[i, q, :, at].astype(F32)

    def partner_far(n):
        at = chunk(n)
        issue(n + 5)
        combine(3, n)
        wait_for(sib.at[3, :, :, at], m_recv.at[3, n])
        for q in range(4):
            zred[3, q, :, at] = summed(3, q, at).astype(BF16)
        send(
            zred.at[3, :, :, at], xfar.at[:, :, at], f_send.at[n], f_recv.at[n], frame=at_x(2)
        )

    def own_far(n):
        at = chunk(n)
        wait_for(sib.at[2, :, :, at], m_recv.at[2, n])
        wait_for(xfar.at[:, :, at], f_recv.at[n])
        for way, (block, step, side, slot) in enumerate(
            ((5, 6, 0, 1), (4, 2, 1, 1), (6, 7, 0, 0), (3, 1, 1, 0))
        ):
            q = (z + block) % 4
            zred[2, q, :, at] = (summed(2, q, at) + xfar[q, :, at].astype(F32)).astype(BF16)
            send(
                zred.at[2, q, :, at], zfar.at[side, slot, :, at], q_send.at[way, n], q_recv.at[n],
                pixel=(z + step) % DEPTH * 2 + c,
            )

    def own_near(n):
        at = chunk(n)
        wait_for(sib.at[0, :, :, at], m_recv.at[0, n])
        wait_for(zfar.at[:, :, :, at], q_recv.at[n])
        for way, block in enumerate((2, 7, 1, 0)):
            q = (z + block) % 4
            total = summed(0, q, at)
            if way < 2:
                for slot in range(2):
                    total = total + zfar[1 - way, slot, :, at].astype(F32)
            zred[0, q, :, at] = total.astype(BF16)
            if way < 3:
                send(
                    zred.at[0, q, :, at], zin.at[way, :, at],
                    nq_send.at[way, n], nq_recv.at[n], pixel=(z + block) % DEPTH * 2 + c,
                )

    def first_far(n):
        issue(n + 3)
        combine(2, n)

    loop(0, 2, first_far)
    loop(0, 4, partner_far)

    def last_far(n):
        issue(n + 7)
        combine(2, n)

    loop(2, 4, last_far)

    loop(0, 3, own_far)

    for side in range(2):
        for part in range(4):
            wait_for(dn_all.at[pl.ds(0, shares[part][-1])], w_send.at[side, part])
    wait_for(s_out.at[:, pl.ds(0, 15)], a_send.at[0])
    wait_for(t_out.at[:, pl.ds(0, 15)], a_send.at[1])
    wait_for(s_part.at[pl.ds(0, 15)], a_send.at[2])
    wait_for(t_part.at[pl.ds(0, 15)], a_send.at[3])
    wait_for(r_in.at[pl.ds(0, 15)], r_send.at[0])
    wait_for(rt.at[0], r_send.at[1])
    wait_for(mine, pair_send.at[0])

    def sent(frame, *blocks):
        for d in blocks:
            wait_for(tok.at[0, 0, 0, 0], z_send.at[frame, d + 3])

    sent(0, -3, -2, -1, 1, 2, 3, 4)
    sent(1, -1, 1, 2)

    @pl.when(c == 1)
    def _():
        sent(1, -3, -2, 3, 4)
        wait_for(tok.at[0, 0, 0], c_send.at[1, 1])


    def sent_groups(i):
        wait_for(tok.at[0, 0, 0], c_send.at[i % 2, i // 2])
        wait_for(rows_out.at[i, pl.ds(0, SIDE - 1)], y_send.at[i])

    loop(0, 3, sent_groups)
    wait_for(rows_out.at[3, pl.ds(0, SIDE - 1), high], y_send.at[3])
    wait_for(arrive.at[3, :, low], pair_send.at[3])

    def sent_parts(n):
        at = chunk(n)
        for i in (2, 3):
            wait_for(parts.at[i, pl.ds(0, SIDE - 1), :, at], b_send.at[i, n])
        wait_for(xin.at[:, :, at], h_send.at[n])

    loop(0, D // CHUNK, sent_parts)

    def last_steps(n):
        issue(n + 11)
        combine(0, n)
        own_near(n)

        @pl.when(n == 0)
        def _():
            own_far(3)

    loop(0, 4, last_steps)

    def sent_chunks(n):
        at = chunk(n)
        for i in (0, 2, 3):
            wait_for(mixed.at[i, 0, :, :, at], m_send.at[i, n])
        wait_for(parts.at[0, pl.ds(0, SIDE - 1), :, at], b_send.at[0, n])
        for way in range(4):
            wait_for(zred.at[0, 0, :, at], q_send.at[way, n])
        wait_for(zred.at[3, :, :, at], f_send.at[n])

    loop(0, D // CHUNK, sent_chunks)

    def finish(n):
        at = chunk(n)
        wait_for(zin.at[:, :, at], nq_recv.at[n])
        result = zred[0, spot, :, at].astype(F32)
        for way in range(3):
            result = result + zin[way, :, at].astype(F32)
        out[1, :, at] = result.astype(BF16)

    loop(0, 4, finish)

    def sent_near(n):
        for way in range(3):
            wait_for(zred.at[0, 0, :, chunk(n)], nq_send.at[way, n])

    loop(0, D // CHUNK, sent_near)


def per_device(
    tokens,
    spatial_inputs,
    temporal_inputs,
    gate_spatial,
    gate_temporal,
    norm_gain,
    route_experts,
    route_weights,
    expert_gate_up,
    expert_down,
):
    vmem = pl.BlockSpec(memory_space=pltpu.VMEM)
    hbm = pl.BlockSpec(memory_space=pl.ANY)
    dma = pltpu.SemaphoreType.DMA

    def buf(*shape, dtype=BF16):
        return pltpu.VMEM(shape, dtype)

    both = pl.pallas_call(
        kernel,
        out_shape=jax.ShapeDtypeStruct((2, HERE, D), BF16),
        in_specs=[hbm] * 3 + [vmem] * 5 + [hbm] * 2,
        out_specs=vmem,
        scratch_shapes=[
            buf(HERE, D), buf(HERE, 3 * D), buf(HERE, 3 * D),
            buf(2 * FF_PAD, D), buf(FF_PAD, D), buf(FF_PAD // GROUP, GROUP, GROUP),
            buf(3, HEADS, HERE, HDIM), buf(3, HEADS, HERE, HDIM),
            buf(3, HEADS, HERE, HDIM), buf(3, HEADS, HERE, HDIM),
            buf(HEADS, HERE, HDIM), buf(HEADS, HERE, HDIM), buf(HERE, D), buf(HERE, D),
            buf(16, 128), buf(16, 16, 128), buf(2, 2, 2, 16, 128),
            buf(2, 2, 2, 4, HERE, D),
            buf(4, GROUP, GROUP), buf(4, GROUP, GROUP),
            buf(4, SIDE, SLOTS, D), buf(4, SIDE, SLOTS, D), buf(4, SIDE, SLOTS, D),
            buf(4, SIDE, SLOTS, D),
            buf(4, 2, 4, HERE, D), buf(4, 4, HERE, D), buf(4, 4, HERE, D),
            buf(3, HERE, D), buf(2, 2, HERE, D), buf(4, HERE, D),
            buf(SIDE, SLOTS, D),
            dma((6,)), dma((2, 4)), dma((2, 4)), dma((4,)), dma((4,)), dma((2,)), dma((2,)),
            dma((4,)), dma((4,)), dma((2, 8)), dma((2, 8)), dma((2, 2)), dma((2, 2)),
            dma((4,)), dma((4,)), dma((4, 4)), dma((4, 4)), dma((4, 4)), dma((4, 4)),
            dma((4, 4)), dma((4,)), dma((4,)), dma((4,)), dma((4,)), dma((4,)), dma((3, 4)), dma((4,)),
        ],
        compiler_params=pltpu.CompilerParams(
            collective_id=0, has_side_effects=True, vmem_limit_bytes=60 * 1024 * 1024
        ),
    )(
        tokens[0],
        spatial_inputs[0],
        temporal_inputs[0],
        gate_spatial[None],
        gate_temporal[None],
        norm_gain[None],
        jnp.transpose(route_experts, (2, 0, 1)),
        jnp.transpose(route_weights, (2, 0, 1)),
        jnp.transpose(expert_gate_up, (0, 2, 1))[0],
        expert_down[0],
    )
    return (both[:1], both[1:])


def solution(mesh):
    in_specs = (
        P("frame", "pixel", None),
        P("frame", "pixel", None),
        P("frame", "pixel", None),
        P(),
        P(),
        P(),
        P("frame", "pixel", None),
        P("frame", "pixel", None),
        P(("frame", "pixel"), None, None),
        P(("frame", "pixel"), None, None),
    )
    out_specs = (P("frame", "pixel", None), P("frame", "pixel", None))
    return jax.shard_map(
        per_device, mesh=mesh, in_specs=in_specs, out_specs=out_specs, check_vma=False
    )
```
